256 devices in a mesh: dp: 32 (over z, x), frame: 8 (over y, core).
Axes of the slice: x: 4, y: 4, z: 8, core: 2. Of those that a mesh axis runs over, the one named last changes fastest.
Arguments:
- queries: bfloat16 [32, 2048, 3072], P('dp', 'frame'), may hold values from -68 to 68
- keys: bfloat16 [32, 2048, 3072], P('dp', 'frame'), may hold values from -4 to 4
- values: bfloat16 [32, 2048, 3072], P('dp', 'frame'), may hold values from -5 to 5
- tokens_in: bfloat16 [32, 2048, 3200], P('dp', 'frame'), may hold values from -6 to 6
- out_weight: bfloat16 [3072, 3200], P(None, 'dp'), may hold values from -0.109375 to 0.109375
- pool_keys: bfloat16 [3200, 16], replicated, may hold values from -0.14495689 to 0.14495689
- proj_weight: float32 [3200, 1024], P('frame'), may hold values from -0.109375 to 0.109375
- captions: float32 [32, 1024], P('dp'), may hold values from -6 to 6
- valid_frames: int32 [32], P('dp'), may hold values from 1 to 16, as said below
Outputs:
- block_out: bfloat16 [32, 2048, 3200], P('dp', 'frame')
- clip_loss: float32 [32], P('dp')
The draws below stay inside these ranges and needn't reach their ends.
Inputs may be any that keep to these rules, and one draw needn't show every extreme that they name: `valid_frames`: every clip has at least one real frame, one clip has all 16, one has a single frame.
All inputs are finite; a program needn't handle non-finite values.
Results may differ from the reference program's by a relative error of at most 0.0029.
Values may be sent and summed in bfloat16 or wider, within the bound.
A program may use at most 128 MiB of HBM per device.

```python
import jax
import jax.numpy as jnp
from jax import lax

D = 3200
HEADS = 24
HD = 128
G = 16
E = 1024
FRAMES = 16
TPF = 128
CLIPS = 32
SEQ = 2048


def shared_keys(key):
    return jnp.clip(jax.random.normal(key, (CLIPS, SEQ, HEADS * HD), jnp.float32), -4.0, 4.0)


def shared_pool(key):
    pool_key = jax.random.fold_in(key, 101)
    spread = 2.0 / jnp.sqrt(jnp.float32(D))
    return jnp.clip(jax.random.normal(pool_key, (D, G), jnp.float32), -4.0, 4.0) * spread


def draw_keys(key, part):
    base = shared_keys(key)
    return base.astype(jnp.bfloat16)


def draw_queries(key, part):
    key = jax.random.fold_in(key, 7)
    fresh = jnp.clip(jax.random.normal(key, (CLIPS, SEQ, HEADS * HD), jnp.float32), -4.0, 4.0)
    return fresh.astype(jnp.bfloat16)


def draw_pool_keys(key, part):
    base = shared_pool(key)
    return base.astype(jnp.bfloat16)


def draw_tokens_in(key, part):
    key = jax.random.fold_in(key, 13)
    fresh = jnp.clip(jax.random.normal(key, (CLIPS, SEQ, D), jnp.float32), -6.0, 6.0)
    return fresh.astype(jnp.bfloat16)


def draw_valid_frames(key, part):
    key = jax.random.fold_in(key, 11)
    counts = jax.random.randint(key, (CLIPS,), 1, FRAMES + 1).astype(jnp.int32)
    counts = counts.at[0].set(FRAMES)
    counts = counts.at[CLIPS - 1].set(1)
    return counts


def block_scale(key, shape, pieces, least, high):
    gain = 1.0
    for axis_at, parts in pieces:
        steps = jax.random.uniform(jax.random.fold_in(jax.random.fold_in(key, 6), axis_at), (parts,), jnp.float32, least / len(pieces), high / len(pieces))
        gain = gain * jnp.repeat(jnp.exp(steps), shape[axis_at] // parts).reshape((-1,) + (1,) * (len(shape) - 1 - axis_at))
    return gain


def normal_values(own_key, dims, deviation, reach, shards=(), kind=jnp.bfloat16):
    drawn = jax.random.normal(own_key, dims, jnp.float32) * deviation
    if len(shards) > 0:
        drawn = block_scale(own_key, dims, shards, -0.22, 0.18) * drawn
    return jnp.clip(drawn, min=-reach, max=reach).astype(kind)


def setup_inputs(seed: int = 0) -> dict:
    arg_keys = jax.random.split(jax.random.key(seed), 10)
    return {
        "queries": draw_queries(jax.random.fold_in(arg_keys[9], 71), 0),
        "keys": draw_keys(jax.random.fold_in(arg_keys[9], 71), 0),
        "values": normal_values(arg_keys[2], (CLIPS, SEQ, HEADS * HD), 1.0, 5.0, ((0, 32), (1, 8))),
        "tokens_in": draw_tokens_in(jax.random.fold_in(arg_keys[9], 71), 0),
        "out_weight": normal_values(arg_keys[4], (HEADS * HD, D), (HEADS * HD) ** -0.5, 0.109375, ((1, 32),)),
        "pool_keys": draw_pool_keys(jax.random.fold_in(arg_keys[9], 71), 0),
        "proj_weight": normal_values(arg_keys[6], (D, E), D ** -0.5, 0.109375, ((0, 8),), jnp.float32),
        "captions": normal_values(arg_keys[7], (CLIPS, E), 1.0, 6.0, ((0, 32),), jnp.float32),
        "valid_frames": draw_valid_frames(jax.random.fold_in(arg_keys[9], 71), 0),
    }


sharpness_factor = 1.0 / 0.07

def attend_clip(query_rows, key_rows, value_rows, keep):
    head_q = query_rows.reshape(SEQ, HEADS, HD).transpose(1, 0, 2)
    head_k = key_rows.reshape(SEQ, HEADS, HD).transpose(1, 0, 2)
    head_v = value_rows.reshape(SEQ, HEADS, HD).transpose(1, 0, 2)

    def one_head(triple):
        qpart, kpart, vpart = triple
        scores = jnp.dot(qpart, kpart.T, preferred_element_type=jnp.float32) / jnp.sqrt(jnp.float32(HD))
        scores = jnp.where(keep[None, :], scores, jnp.float32(-1e+30))
        weights = jax.nn.softmax(scores, axis=-1).astype(jnp.bfloat16)
        return jnp.dot(weights, vpart, preferred_element_type=jnp.float32).astype(jnp.bfloat16)
    outputs = lax.map(one_head, (head_q, head_k, head_v))
    return outputs.transpose(1, 0, 2).reshape(SEQ, HEADS * HD)

def reference(queries, keys, values, tokens_in, out_weight, pool_keys, proj_weight, captions, valid_frames):

    def one_clip(items):
        query_rows, key_rows, value_rows, residual, count = items
        keep = jnp.arange(SEQ, dtype=jnp.int32) // TPF < count
        attended = attend_clip(query_rows, key_rows, value_rows, keep)
        block = (residual.astype(jnp.float32) + jnp.dot(attended, out_weight, preferred_element_type=jnp.float32)).astype(jnp.bfloat16)
        scores = jnp.dot(block, pool_keys, preferred_element_type=jnp.float32)
        scores = jnp.where(keep[:, None], scores, jnp.float32(-1e+30))
        weights = jax.nn.softmax(scores, axis=0)
        grouped = block.astype(jnp.float32).reshape(SEQ, G, D // G)
        pooled = jnp.einsum('tg,tgd->gd', weights, grouped, precision=lax.Precision.HIGHEST)
        embed = jnp.dot(pooled.reshape(D), proj_weight, precision=lax.Precision.HIGHEST)
        return (block, embed)
    block_out, clip_raw = lax.map(one_clip, (queries, keys, values, tokens_in, valid_frames))
    video_segment_features = clip_raw / jnp.sqrt(lax.optimization_barrier(jnp.sum(clip_raw * clip_raw, axis=-1, keepdims=True)) + 1e-06)
    sentence_embedding_matrix = captions / jnp.sqrt(lax.optimization_barrier(jnp.sum(captions * captions, axis=-1, keepdims=True)) + 1e-06)
    affinity_score_matrix = sharpness_factor * jnp.dot(video_segment_features, sentence_embedding_matrix.T, precision=lax.Precision.HIGHEST)
    aligned_couples = jnp.diagonal(affinity_score_matrix)
    row_lse = jax.scipy.special.logsumexp(affinity_score_matrix, axis=1)
    col_lse = jax.scipy.special.logsumexp(affinity_score_matrix, axis=0)
    clip_loss = 0.5 * (row_lse - aligned_couples) + 0.5 * (col_lse - aligned_couples)
    return (block_out, clip_loss)
```

```python
import functools

import jax
import jax.numpy as jnp
from jax import lax
from jax.experimental import pallas as pl
from jax.experimental.pallas import tpu as pltpu
from jax.sharding import PartitionSpec as P

D = 3200
HEADS = 24
HD = 128
G = 16
TPF = 128
SEQ = 2048
TOK = 256
ROUNDS = 3
NF = 8
NZ = 8
NX = 4
KR = NF * HD
PIECE = 100
PAD = 128
WIDE = NZ * NX * PAD
XPART = 224
ZPART = 288
SCALE = 1.4426950408889634 / (128.0**0.5)
SHARP = 1.0 / 0.07

MESH = pl.DeviceIdType.MESH
F32 = jnp.float32
BF16 = jnp.bfloat16


def nt_dot(a, b):
    return lax.dot_general(a, b, (((1,), (1,)), ((), ())), preferred_element_type=F32)


def body(
    q_hbm, k_hbm, v_hbm, tok_hbm, w_hbm, pk_ref, proj_hbm, cap_ref, valid_ref,
    out_hbm, loss_ref,
    tok, wown, proj, projp, wbuf, qkv, k2, vext, osend, orecv, acc, blk, outv,
    msg, parts, emb, embs, caps, logit,
    lsem, qs, qr, os_, or_, z1s, z1r, z2s, z2r, x1s, x1r, x2s, x2r, sbs, sbr,
    cs, cr, ms, mr, es, er, gs, gr,
):
    dp = lax.axis_index("dp")
    f = lax.axis_index("frame")
    z = dp // NX
    x = lax.rem(dp, NX)
    c = lax.rem(f, 2)
    sib = f + 1 - 2 * c
    sign = 1 - 2 * c
    valid = valid_ref[0]

    def at_z(zz):
        return {"dp": zz * NX + x}

    def at_x(xx):
        return {"dp": z * NX + xx}

    def remote(src, dst, ssem, rsem, where):
        return pltpu.make_async_remote_copy(
            src_ref=src, dst_ref=dst, send_sem=ssem, recv_sem=rsem, device_id=where, device_id_type=MESH
        )

    loads = [
        pltpu.make_async_copy(w_hbm, wown, lsem.at[0]),
        pltpu.make_async_copy(tok_hbm, tok, lsem.at[1]),
        pltpu.make_async_copy(proj_hbm, proj, lsem.at[2]),
    ]
    for load in loads:
        load.start()

    barrier = pltpu.get_barrier_semaphore()
    for i in range(1, NF):
        pl.semaphore_signal(barrier, inc=1, device_id={"frame": lax.rem(f + i, NF)}, device_id_type=MESH)
    for i in range(1, NX):
        pl.semaphore_signal(barrier, inc=1, device_id=at_x(lax.rem(x + i, NX)), device_id_type=MESH)
    for i in range(1, NZ):
        pl.semaphore_signal(barrier, inc=1, device_id=at_z(lax.rem(z + i, NZ)), device_id_type=MESH)

    loads[0].wait()
    for r in range(ROUNDS):
        rows = pl.ds(pl.multiple_of(r * KR + c * 512, 512), 512)
        wbuf[z, x, rows, :] = jnp.zeros((512, PAD), BF16)
        wbuf[z, x, rows, 0:PIECE] = wown[rows, :]
    pl.semaphore_wait(barrier, NF - 1 + NX - 1 + NZ - 1)

    def xrows(r, core):
        return pl.ds(pl.multiple_of(r * KR + core * 512, 16), XPART)

    def zrows(r, core):
        return pl.ds(pl.multiple_of(r * KR + core * 512 + XPART, 16), ZPART)

    sends = []

    def go(copy):
        copy.start()
        sends.append(copy)

    def zturn(way, step):
        s = sign if way == 0 else -sign
        return lax.rem(z - s * step + NZ, NZ)

    def znext(way):
        s = sign if way == 0 else -sign
        return lax.rem(z + s + NZ, NZ)

    LAST = (4, 3)

    def z2_block(r, zb):
        return wbuf.at[zb, x, zrows(r, c), :]

    def z1_block(r, zb):
        return wbuf.at[zb, :, xrows(r, c), :]

    def z_copy(block, r, way, step, ss, rs):
        ref = block(r, zturn(way, step))
        return remote(ref, ref, ss.at[r, way, step], rs.at[r, way, step], at_z(znext(way)))

    def z_send(block, r, step, ss, rs):
        for way in range(2):
            if step < LAST[way]:
                go(z_copy(block, r, way, step, ss, rs))

    def z_step(block, r, step, ss, rs):
        for way in range(2):
            if step <= LAST[way]:
                ref = block(r, zturn(way, step))
                remote(ref, ref, ss.at[r, way, step - 1], rs.at[r, way, step - 1], at_z(znext(way))).wait_recv()
                if step < LAST[way]:
                    go(z_copy(block, r, way, step, ss, rs))

    def z2_start(r):
        z_send(z2_block, r, 0, z2s, z2r)

    def z2_step(r, step):
        z_step(z2_block, r, step, z2s, z2r)

    def z1_start(r):
        z_send(z1_block, r, 0, z1s, z1r)

    def z1_step(r, step):
        z_step(z1_block, r, step, z1s, z1r)

    def x1_copy(r, i, xx):
        ref = wbuf.at[z, xx, xrows(r, c), :]
        return remote(ref, ref, x1s.at[r, i - 1], x1r.at[r, i - 1], at_x(lax.rem(x + i, NX)))

    def x1_start(r):
        for i in range(1, NX):
            go(x1_copy(r, i, x))

    def x1_wait(r):
        for i in range(1, NX):
            x1_copy(r, i, lax.rem(x - i + NX, NX)).wait_recv()

    right = lax.rem(x + 1, NX)
    left = lax.rem(x + NX - 1, NX)
    across = lax.rem(x + 2, NX)

    def x2_copy(r, which, xx):
        part = (pl.ds(0, NZ), pl.ds(0, NZ), pl.ds(0, 4), pl.ds(4, 4))[which]
        ref = wbuf.at[part, xx, zrows(r, c), :]
        to = (right, left, right, left)[which]
        return remote(ref, ref, x2s.at[r, which], x2r.at[r, which], at_x(to))

    def x2_start(r):
        go(x2_copy(r, 0, x))
        go(x2_copy(r, 1, x))

    def x2_forward(r):
        x2_copy(r, 0, left).wait_recv()
        go(x2_copy(r, 2, left))
        x2_copy(r, 1, right).wait_recv()
        go(x2_copy(r, 3, right))

    def x2_finish(r):
        x2_copy(r, 2, across).wait_recv()
        x2_copy(r, 3, across).wait_recv()

    def sib_copy(r, which, core):
        ref = wbuf.at[:, :, (xrows, zrows)[which](r, core), :]
        return remote(ref, ref, sbs.at[r, which], sbr.at[r, which], {"frame": sib})

    def sib_start(r, which):
        go(sib_copy(r, which, c))

    def sib_wait(r):
        for which in range(2):
            sib_copy(r, which, 1 - c).wait_recv()

    def qkv_start(r):
        for i in range(1, NF):
            t = lax.rem(f + i, NF)
            cols = pl.ds(pl.multiple_of((r * NF + t) * HD, HD), HD)
            for a, ref in enumerate((k_hbm, v_hbm, q_hbm)):
                remote(
                    ref.at[:, cols],
                    qkv.at[r, a, pl.ds(pl.multiple_of(f * TOK, TOK), TOK), :],
                    qs.at[r], qr.at[r], {"frame": t},
                ).start()
        cols = pl.ds(pl.multiple_of((r * NF + f) * HD, HD), HD)
        for a, ref in enumerate((k_hbm, v_hbm, q_hbm)):
            pltpu.make_async_copy(
                ref.at[:, cols], qkv.at[r, a, pl.ds(pl.multiple_of(f * TOK, TOK), TOK), :], qr.at[r]
            ).start()

    def qkv_wait(r):
        pltpu.make_async_copy(qkv.at[r], qkv.at[r], qr.at[r]).wait()

    def attend(r):
        qkv_wait(r)
        for i in range(8):
            rows = slice(256 * i, 256 * (i + 1))
            live = (lax.broadcasted_iota(jnp.int32, (256, HD), 0) + 256 * i) // TPF < valid
            kk = qkv[r, 0, rows, :].astype(F32)
            first = qkv[r, 0, 0:16, :].astype(F32)[0:1, :]
            kk = jnp.where(live, kk, jnp.broadcast_to(first, (256, HD))) * SCALE
            hi = kk.astype(BF16)
            k2[rows, 0:HD] = hi
            k2[rows, HD : 2 * HD] = (kk - hi.astype(F32)).astype(BF16)
            vext[rows, 0:HD] = jnp.where(live, qkv[r, 1, rows, :].astype(F32), 0.0).astype(BF16)
            vext[rows, HD : 2 * HD] = jnp.where(live, 1.0, 0.0).astype(BF16)

        def block(i, carry):
            b = lax.rem(f + 1 + i, NF)
            qq = qkv[r, 2, pl.ds(pl.multiple_of(b * TOK, TOK), TOK), :]
            scores = nt_dot(jnp.concatenate([qq, qq], axis=1), k2[...])
            peak = jnp.max(scores, axis=1, keepdims=True)
            weights = jnp.exp2(scores - peak).astype(BF16)
            both = jnp.dot(weights, vext[...], preferred_element_type=F32)
            osend[r, b] = (both[:, 0:HD] / both[:, HD : 2 * HD]).astype(BF16)
            cols = pl.ds(pl.multiple_of(r * KR + f * HD, HD), HD)

            @pl.when(i < NF - 1)
            def _():
                remote(osend.at[r, b], orecv.at[:, cols], os_.at[r], or_.at[r], {"frame": b}).start()

            @pl.when(i == NF - 1)
            def _():
                pltpu.make_async_copy(osend.at[r, b], orecv.at[:, cols], or_.at[r]).start()

            return carry

        lax.fori_loop(0, NF, block, 0)

    def attended_wait(r):
        cols = orecv.at[:, pl.ds(r * KR, KR)]
        pltpu.make_async_copy(cols, cols, or_.at[r]).wait()

    def project(r):
        def step(zz, carry):
            for pair in range(2):
                rows = pl.ds(r * KR, KR)
                rhs = jnp.concatenate([wbuf[zz, 2 * pair, rows, :], wbuf[zz, 2 * pair + 1, rows, :]], axis=1)
                cols = pl.ds(pl.multiple_of(zz * 512 + pair * 256, 256), 256)
                total = acc[:, cols] + jnp.dot(
                    orecv[:, r * KR : (r + 1) * KR], rhs, preferred_element_type=F32
                )
                if r < ROUNDS - 1:
                    acc[:, cols] = total
                else:
                    blk[:, cols] = total.astype(BF16)
            return carry

        lax.fori_loop(0, NZ, step, 0)

    for r in range(ROUNDS):
        z2_start(r)
        x1_start(r)
        qkv_start(r)

    for n in range(8):
        emb[0, n : n + 1, :] = cap_ref[0:1, 128 * n : 128 * (n + 1)]
    own_cap = emb[0]
    norm = jnp.sqrt(jnp.sum(own_cap * own_cap, keepdims=True) + 1e-06)
    caps[z, x] = own_cap / norm
    cap_sends = []

    def cap_x(i, xx):
        ref = caps.at[z, xx]
        return remote(ref, ref, cs.at[i - 1], cr.at[i - 1], at_x(lax.rem(x + i, NX)))

    def cap_z(i, zz):
        ref = caps.at[zz]
        return remote(ref, ref, cs.at[NX - 2 + i], cr.at[NX - 2 + i], at_z(lax.rem(z + i, NZ)))

    for i in range(1, NX):
        go(cap_x(i, x))

    loads[1].wait()
    for j in range(NZ * NX):
        acc[:, PAD * j : PAD * (j + 1)] = jnp.zeros((TOK, PAD), F32)
        acc[:, PAD * j : PAD * j + PIECE] = tok[:, PIECE * j : PIECE * (j + 1)].astype(F32)

    for step in range(1, 5):
        z2_step(0, step)
    x2_start(0)
    x1_wait(0)
    z1_start(0)

    for i in range(1, NX):
        cap_x(i, lax.rem(x - i + NX, NX)).wait_recv()
    for i in range(1, NZ):
        go(cap_z(i, z))

    loads[2].wait()
    projp[...] = jnp.zeros((512, 1024), F32)
    for i in range(4):
        projp[PAD * i : PAD * i + PIECE, :] = proj[PIECE * i : PIECE * (i + 1), :]

    for step in range(1, 5):
        z2_step(1, step)
    x2_forward(0)
    x2_start(1)
    for step in range(1, 5):
        z1_step(0, step)
    x1_wait(1)
    z1_start(1)

    attend(0)

    sib_start(0, 0)
    x2_finish(0)
    sib_start(0, 1)
    for step in range(1, 5):
        z2_step(2, step)
    x2_forward(1)
    x2_start(2)
    for step in range(1, 5):
        z1_step(1, step)
    x1_wait(2)
    z1_start(2)

    attend(1)

    sib_start(1, 0)
    x2_finish(1)
    sib_start(1, 1)

    attend(2)

    sib_wait(0)
    attended_wait(0)
    project(0)
    x2_forward(2)
    for step in range(1, 5):
        z1_step(2, step)
    sib_start(2, 0)
    sib_wait(1)
    attended_wait(1)
    project(1)
    x2_finish(2)
    sib_start(2, 1)
    for i in range(1, NZ):
        cap_z(i, lax.rem(z - i + NZ, NZ)).wait_recv()
    sib_wait(2)
    attended_wait(2)
    project(2)

    scores = nt_dot(pk_ref[...], blk[...])
    token = lax.broadcasted_iota(jnp.int32, (G, TOK), 1) + f * TOK
    live = token // TPF < valid
    masked = jnp.where(live, scores, -1e30)
    peak = jnp.max(masked, axis=1, keepdims=True)
    expo = jnp.where(live, jnp.exp(masked - peak), 0.0)
    total = jnp.sum(expo, axis=1, keepdims=True)
    e0 = expo.astype(BF16)
    rest = expo - e0.astype(F32)
    e1 = rest.astype(BF16)
    e2 = (rest - e1.astype(F32)).astype(BF16)
    w48 = jnp.dot(jnp.concatenate([e0, e1, e2], axis=0), blk[...], preferred_element_type=F32)
    w16 = w48[0:G] + w48[G : 2 * G] + w48[2 * G : 3 * G]
    mine = lax.broadcasted_iota(jnp.int32, (G, WIDE), 1) // (2 * PAD) == lax.broadcasted_iota(jnp.int32, (G, WIDE), 0)

    def spread(value):
        return jnp.sum(jnp.where(mine, value, 0.0), axis=0, keepdims=True)

    msg[0:1, :] = spread(w16)
    msg[1:2, :] = spread(jnp.broadcast_to(peak, (G, WIDE)))
    msg[2:3, :] = spread(jnp.broadcast_to(total, (G, WIDE)))
    msg[3:8, :] = jnp.zeros((5, WIDE), F32)

    def part_copy(i, src):
        t = lax.rem(f + i, NF)
        return remote(
            msg.at[:, pl.ds(pl.multiple_of(t * 512, 512), 512)], parts.at[src],
            ms.at[i - 1], mr.at[i - 1], {"frame": t},
        )

    for i in range(1, NF):
        go(part_copy(i, f))
    parts[f] = msg[:, pl.ds(pl.multiple_of(f * 512, 512), 512)]

    for j in range(NZ * NX):
        outv[:, PIECE * j : PIECE * (j + 1)] = blk[:, PAD * j : PAD * j + PIECE]
    store = pltpu.make_async_copy(outv, out_hbm, lsem.at[0])
    store.start()

    for i in range(1, NF):
        part_copy(i, lax.rem(f - i + NF, NF)).wait_recv()
    gathered = parts[...]
    peaks = gathered[:, 1, :]
    top = jnp.max(peaks, axis=0, keepdims=True)
    scale = jnp.exp(peaks - top)
    denominator = jnp.sum(gathered[:, 2, :] * scale, axis=0, keepdims=True)
    pooled = jnp.sum(gathered[:, 0, :] * scale, axis=0, keepdims=True) / denominator
    column = jnp.transpose(jnp.broadcast_to(pooled, (PAD, 512)))
    for n in range(8):
        emb[0, n : n + 1, :] = jnp.sum(column * projp[:, 128 * n : 128 * (n + 1)], axis=0, keepdims=True)

    def emb_copy(i, src):
        return remote(emb.at[0], embs.at[src], es.at[i - 1], er.at[i - 1], {"frame": lax.rem(f + i, NF)})

    for i in range(1, NF):
        go(emb_copy(i, f))
    embs[f] = emb[0]
    for i in range(1, NF):
        emb_copy(i, lax.rem(f - i + NF, NF)).wait_recv()
    raw = jnp.sum(embs[...], axis=0)
    clip = raw / jnp.sqrt(jnp.sum(raw * raw, keepdims=True) + 1e-06)

    products = jnp.sum(caps[...].reshape(NZ * NX, 8, 128) * clip[None], axis=1)
    square = jnp.concatenate([products, jnp.zeros((96, 128), F32)], axis=0)
    row = SHARP * jnp.sum(jnp.transpose(square), axis=0, keepdims=True)
    logit[z, x] = jnp.broadcast_to(row, (8, 128))

    def log_x(i, xx):
        ref = logit.at[z, xx]
        return remote(ref, ref, gs.at[i - 1], gr.at[i - 1], at_x(lax.rem(x + i, NX)))

    def log_z(i, zz):
        ref = logit.at[zz]
        return remote(ref, ref, gs.at[NX - 2 + i], gr.at[NX - 2 + i], at_z(lax.rem(z + i, NZ)))

    for i in range(1, NX):
        go(log_x(i, x))
    lane = lax.broadcasted_iota(jnp.int32, (1, 128), 1)
    own = jnp.where(lane < NZ * NX, row, -jnp.inf)
    own_top = jnp.max(own, axis=1, keepdims=True)
    row_lse = jnp.log(jnp.sum(jnp.exp(own - own_top), axis=1, keepdims=True)) + own_top
    for i in range(1, NX):
        log_x(i, lax.rem(x - i + NX, NX)).wait_recv()
    for i in range(1, NZ):
        go(log_z(i, z))
    for i in range(1, NZ):
        log_z(i, lax.rem(z - i + NZ, NZ)).wait_recv()
    table = logit[...].reshape(NZ * NX, 8, 128)
    col_top = jnp.max(table, axis=0)
    col_lse = (jnp.log(jnp.sum(jnp.exp(table - col_top[None]), axis=0)) + col_top)[0:1, :]
    picked = jnp.where(lane == dp, 0.5 * col_lse - row, 0.0)
    value = 0.5 * row_lse + jnp.sum(picked, axis=1, keepdims=True)
    loss_ref[...] = jnp.broadcast_to(value, (1, 128))

    for copy in sends:
        copy.wait_send()
    for r in range(ROUNDS):
        away = qkv.at[r, :, pl.ds(0, SEQ - TOK), :]
        pltpu.make_async_copy(away, away, qs.at[r]).wait()
        away = orecv.at[:, pl.ds(0, KR - HD)]
        pltpu.make_async_copy(away, away, os_.at[r]).wait()
    store.wait()


def local(
    queries, keys, values, tokens_in, out_weight, pool_keys, proj_weight, captions, valid_frames
):
    pool = jnp.pad(pool_keys.reshape(NZ * NX, PIECE, G), ((0, 0), (0, PAD - PIECE), (0, 0))).reshape(WIDE, G).T
    any_ = pl.BlockSpec(memory_space=pl.ANY)
    vmem = pl.BlockSpec(memory_space=pltpu.VMEM)
    smem = pl.BlockSpec(memory_space=pltpu.SMEM)
    dma = pltpu.SemaphoreType.DMA
    block_out, loss = pl.pallas_call(
        body,
        out_shape=(
            jax.ShapeDtypeStruct((TOK, D), BF16),
            jax.ShapeDtypeStruct((1, 128), F32),
        ),
        in_specs=[any_, any_, any_, any_, any_, vmem, any_, vmem, smem],
        out_specs=(any_, vmem),
        scratch_shapes=[
            pltpu.VMEM((TOK, D), BF16),
            pltpu.VMEM((HEADS * HD, PIECE), BF16),
            pltpu.VMEM((400, 1024), F32),
            pltpu.VMEM((512, 1024), F32),
            pltpu.VMEM((NZ, NX, HEADS * HD, PAD), BF16),
            pltpu.VMEM((ROUNDS, 3, SEQ, HD), BF16),
            pltpu.VMEM((SEQ, 2 * HD), BF16),
            pltpu.VMEM((SEQ, 2 * HD), BF16),
            pltpu.VMEM((ROUNDS, NF, TOK, HD), BF16),
            pltpu.VMEM((TOK, HEADS * HD), BF16),
            pltpu.VMEM((TOK, WIDE), F32),
            pltpu.VMEM((TOK, WIDE), BF16),
            pltpu.VMEM((TOK, D), BF16),
            pltpu.VMEM((8, WIDE), F32),
            pltpu.VMEM((NF, 8, 512), F32),
            pltpu.VMEM((1, 8, 128), F32),
            pltpu.VMEM((NF, 8, 128), F32),
            pltpu.VMEM((NZ, NX, 8, 128), F32),
            pltpu.VMEM((NZ, NX, 8, 128), F32),
            dma((3,)),
            dma((ROUNDS,)), dma((ROUNDS,)),
            dma((ROUNDS,)), dma((ROUNDS,)),
            dma((ROUNDS, 2, 4)), dma((ROUNDS, 2, 4)),
            dma((ROUNDS, 2, 4)), dma((ROUNDS, 2, 4)),
            dma((ROUNDS, 3)), dma((ROUNDS, 3)),
            dma((ROUNDS, 4)), dma((ROUNDS, 4)),
            dma((ROUNDS, 2)), dma((ROUNDS, 2)),
            dma((10,)), dma((10,)),
            dma((7,)), dma((7,)),
            dma((7,)), dma((7,)),
            dma((10,)), dma((10,)),
        ],
        compiler_params=pltpu.CompilerParams(
            collective_id=0, has_side_effects=True, vmem_limit_bytes=60 * 2**20
        ),
    )(
        queries[0], keys[0], values[0], tokens_in[0], out_weight, pool, proj_weight, captions, valid_frames
    )
    return block_out[None], loss[0, 0:1]


def solution(mesh):
    placed = (
        P("dp", "frame", None),
        P("dp", "frame", None),
        P("dp", "frame", None),
        P("dp", "frame", None),
        P(None, "dp"),
        P(),
        P("frame", None),
        P("dp", None),
        P("dp"),
    )
    return jax.shard_map(
        local,
        mesh=mesh,
        in_specs=placed,
        out_specs=(P("dp", "frame", None), P("dp")),
        check_vma=False,
    )
```

```python
import functools

import jax
import jax.numpy as jnp
from jax import lax
from jax.experimental import pallas as pl
from jax.experimental.pallas import tpu as pltpu
from jax.sharding import PartitionSpec as P

D = 3200
HEADS = 24
HD = 128
G = 16
TPF = 128
SEQ = 2048
TOK = 256
ROUNDS = 3
NF = 8
NZ = 8
NX = 4
KR = NF * HD
PIECE = 100
SCALE = 1.4426950408889634 / (128.0**0.5)
SHARP = 1.0 / 0.07

MESH = pl.DeviceIdType.MESH
F32 = jnp.float32
BF16 = jnp.bfloat16


def nt_dot(a, b):
    return lax.dot_general(a, b, (((1,), (1,)), ((), ())), preferred_element_type=F32)


def body(
    q_hbm, k_hbm, v_hbm, tok_hbm, w_hbm, pk_ref, proj_hbm, cap_ref, valid_ref,
    out_hbm, loss_ref,
    tok, wown, proj, own_a, own_x, stage_a, stage_x, m32, wt, qkv, k2, vext, osend, orecv, acc, blk,
    msg, pout, parts, emb, embs, caps, logit,
    lsem, qs, qr, os_, or_, as_, ar, x1s, x1r, z1s, z1r, z2s, z2r, x2s, x2r, x2f, sbs, sbr,
    cs, cr, ms, mr, es, er, gs, gr,
):
    dp = lax.axis_index("dp")
    f = lax.axis_index("frame")
    z = dp // NX
    x = lax.rem(dp, NX)
    c = lax.rem(f, 2)
    sib = f + 1 - 2 * c
    sign = 1 - 2 * c
    valid = valid_ref[0]
    right = lax.rem(x + 1, NX)
    left = lax.rem(x + NX - 1, NX)
    across = lax.rem(x + 2, NX)

    def at_z(zz):
        return {"dp": zz * NX + x}

    def at_x(xx):
        return {"dp": z * NX + xx}

    def remote(src, dst, ssem, rsem, where):
        return pltpu.make_async_remote_copy(
            src_ref=src, dst_ref=dst, send_sem=ssem, recv_sem=rsem, device_id=where, device_id_type=MESH
        )

    def sent(ref, sem):
        pltpu.make_async_copy(ref, ref, sem).wait()

    loads = [
        pltpu.make_async_copy(w_hbm, wown, lsem.at[0]),
        pltpu.make_async_copy(tok_hbm, tok, lsem.at[1]),
        pltpu.make_async_copy(proj_hbm, proj, lsem.at[2]),
    ]
    for load in loads:
        load.start()

    barrier = pltpu.get_barrier_semaphore()
    for i in range(1, NF):
        pl.semaphore_signal(barrier, inc=1, device_id={"frame": lax.rem(f + i, NF)}, device_id_type=MESH)
    for i in range(1, NX):
        pl.semaphore_signal(barrier, inc=1, device_id=at_x(lax.rem(x + i, NX)), device_id_type=MESH)
    for i in range(1, NZ):
        pl.semaphore_signal(barrier, inc=1, device_id=at_z(lax.rem(z + i, NZ)), device_id_type=MESH)

    half = pl.multiple_of(c * 512, 512)
    loads[0].wait()
    for to in range(NX):
        for tile in range(2):
            lanes = pl.ds(pl.multiple_of((tile + 1) * KR + half + to * 128, 128), 128)
            own_a[to, 0:PIECE, 128 * tile : 128 * (tile + 1)] = wown[:, lanes]
    own_x[0:PIECE, :] = wown[:, pl.ds(half, 512)]
    for to in range(NX):
        own_a[to, 96:112, :] = jnp.concatenate([own_a[to, 96:112, :][0:4], jnp.zeros((12, 256), BF16)], axis=0)
    own_x[96:112, :] = jnp.concatenate([own_x[96:112, :][0:4], jnp.zeros((12, 512), BF16)], axis=0)
    pl.semaphore_wait(barrier, NF - 1 + NX - 1 + NZ - 1)

    def a_copy(i, src):
        to = lax.rem(x + i, NX)
        return remote(own_a.at[to], stage_a.at[src], as_, ar.at[i - 1], at_x(to))

    def x1_copy(i, src):
        return remote(own_x, stage_x.at[src], x1s, x1r.at[i - 1], at_x(lax.rem(x + i, NX)))

    def owner_lanes(tile, xx):
        return pl.ds(pl.multiple_of((tile + 1) * KR + half + xx * 128, 128), 128)

    def half_lanes(h):
        return pl.ds(pl.multiple_of(half + 256 * h, 256), 256)

    def block_rows(zb):
        return pl.ds(pl.multiple_of(400 * zb, 16), 400)

    def zmove(way, step):
        s = sign if way == 0 else -sign
        return lax.rem(z - s * step + NZ, NZ)

    def znext(way):
        s = sign if way == 0 else -sign
        return lax.rem(z + s + NZ, NZ)

    LAST = (4, 3)

    def z2_copy(tile, way, step):
        ref = wt.at[block_rows(zmove(way, step)), owner_lanes(tile, x)]
        return remote(ref, ref, z2s, z2r.at[tile, way, step], at_z(znext(way)))

    def z2_in(tile, way, step):
        ref = wt.at[block_rows(zmove(way, step)), owner_lanes(tile, x)]
        return remote(ref, ref, z2s, z2r.at[tile, way, step - 1], at_z(znext(way)))

    def z1_copy(h, way, step):
        ref = wt.at[block_rows(zmove(way, step)), half_lanes(h)]
        return remote(ref, ref, z1s, z1r.at[h, way, step], at_z(znext(way)))

    def z1_in(h, way, step):
        ref = wt.at[block_rows(zmove(way, step)), half_lanes(h)]
        return remote(ref, ref, z1s, z1r.at[h, way, step - 1], at_z(znext(way)))

    def place(o):
        return zmove(0, (o + 1) // 2) if o % 2 else zmove(1, o // 2)

    def x2_copy(tile, way, o, xx):
        ref = wt.at[block_rows(place(o)), owner_lanes(tile, xx)]
        return remote(ref, ref, x2s, x2r.at[tile, way, o], at_x(right if way == 0 else left))

    def x2_forward_copy(tile, way, o, xx):
        ref = wt.at[block_rows(place(o)), owner_lanes(tile, xx)]
        return remote(ref, ref, x2s, x2f.at[tile, o], at_x(right if way == 0 else left))

    def x2_own(tile, o):
        x2_copy(tile, 0, o, x).start()
        x2_copy(tile, 1, o, x).start()

    def x2_forward(tile, o):
        way, xx = ((0, left), (1, right))[o % 2]
        x2_copy(tile, way, o, xx).wait_recv()
        x2_forward_copy(tile, way, o, xx).start()

    def x2_near(tile):
        for o in range(NZ):
            way, xx = ((1, right), (0, left))[o % 2]
            x2_copy(tile, way, o, xx).wait_recv()

    def x2_far(tile):
        for o in range(NZ):
            x2_forward_copy(tile, o % 2, o, across).wait_recv()

    def z2_start(tile):
        for way in range(2):
            z2_copy(tile, way, 0).start()
        x2_own(tile, 0)

    def z2_step(tile, step):
        for way in range(2):
            if step <= LAST[way]:
                z2_in(tile, way, step).wait_recv()
                if step < LAST[way]:
                    z2_copy(tile, way, step).start()
                x2_own(tile, 2 * step - 1 if way == 0 else 2 * step)

    def z1_start(h):
        for way in range(2):
            z1_copy(h, way, 0).start()

    def z1_step(h, step):
        for way in range(2):
            if step <= LAST[way]:
                z1_in(h, way, step).wait_recv()
                if step < LAST[way]:
                    z1_copy(h, way, step).start()

    def sib_copy(which, core):
        base = core * 512
        if which == 0:
            lanes = pl.ds(pl.multiple_of(base, 512), 512)
        elif which == 1:
            lanes = pl.ds(pl.multiple_of(KR + base, 512), 512)
        else:
            xx = (x, left, right, across)[which - 2]
            lanes = pl.ds(pl.multiple_of(2 * KR + base + xx * 128, 128), 128)
        ref = wt.at[:, lanes]
        return remote(ref, ref, sbs, sbr.at[which], {"frame": sib})

    def sib_start(which):
        sib_copy(which, c).start()

    def sib_wait(which):
        sib_copy(which, 1 - c).wait_recv()

    def merge_a():
        stage_a[x] = own_a[x]
        for i in range(1, NX):
            a_copy(i, lax.rem(x - i + NX, NX)).wait_recv()
        for i in range(NX):
            m32[PIECE * i : PIECE * i + 112, 0:256] = stage_a[i].astype(F32)
        for tile in range(2):
            wt[block_rows(z), owner_lanes(tile, x)] = m32[0:400, 128 * tile : 128 * (tile + 1)].astype(BF16)

    def merge_x():
        stage_x[x] = own_x[...]
        for i in range(1, NX):
            x1_copy(i, lax.rem(x - i + NX, NX)).wait_recv()
        for i in range(NX):
            m32[PIECE * i : PIECE * i + 112, :] = stage_x[i].astype(F32)
        wt[block_rows(z), pl.ds(half, 512)] = m32[0:400, :].astype(BF16)

    def qkv_start(r):
        for i in range(1, NF):
            t = lax.rem(f + i, NF)
            cols = pl.ds(pl.multiple_of((r * NF + t) * HD, HD), HD)
            for a, ref in enumerate((k_hbm, v_hbm, q_hbm)):
                remote(
                    ref.at[:, cols],
                    qkv.at[r, a, pl.ds(pl.multiple_of(f * TOK, TOK), TOK), :],
                    qs.at[r], qr.at[r], {"frame": t},
                ).start()
        cols = pl.ds(pl.multiple_of((r * NF + f) * HD, HD), HD)
        for a, ref in enumerate((k_hbm, v_hbm, q_hbm)):
            pltpu.make_async_copy(
                ref.at[:, cols], qkv.at[r, a, pl.ds(pl.multiple_of(f * TOK, TOK), TOK), :], qr.at[r]
            ).start()

    def qkv_wait(r):
        pltpu.make_async_copy(qkv.at[r], qkv.at[r], qr.at[r]).wait()

    def prepare(r):
        for i in range(8):
            rows = slice(256 * i, 256 * (i + 1))
            live = (lax.broadcasted_iota(jnp.int32, (256, HD), 0) + 256 * i) // TPF < valid
            kk = qkv[r, 0, rows, :].astype(F32)
            first = qkv[r, 0, 0:16, :].astype(F32)[0:1, :]
            kk = jnp.where(live, kk, jnp.broadcast_to(first, (256, HD))) * SCALE
            hi = kk.astype(BF16)
            k2[rows, 0:HD] = hi
            k2[rows, HD : 2 * HD] = (kk - hi.astype(F32)).astype(BF16)
            vext[rows, 0:HD] = jnp.where(live, qkv[r, 1, rows, :].astype(F32), 0.0).astype(BF16)
            vext[rows, HD : 2 * HD] = jnp.where(live, 1.0, 0.0).astype(BF16)

    def attend(r, group):
        heads = pl.ds(pl.multiple_of(r * KR + f * HD, HD), HD)
        for g in range(0, NF, group):
            for i in range(g, g + group):
                b = lax.rem(f + 1 + i, NF)
                qq = qkv[r, 2, pl.ds(pl.multiple_of(b * TOK, TOK), TOK), :]
                scores = nt_dot(jnp.concatenate([qq, qq], axis=1), k2[...])
                peak = jnp.max(scores, axis=1, keepdims=True)
                weights = jnp.exp2(scores - peak).astype(BF16)
                both = jnp.dot(weights, vext[...], preferred_element_type=F32)
                osend[r, b] = (both[:, 0:HD] / both[:, HD : 2 * HD]).astype(BF16)
            for i in range(g, g + group):
                b = lax.rem(f + 1 + i, NF)
                if i < NF - 1:
                    remote(osend.at[r, b], orecv.at[:, heads], os_.at[r], or_.at[r], {"frame": b}).start()
                else:
                    pltpu.make_async_copy(osend.at[r, b], orecv.at[:, heads], or_.at[r]).start()

    def attended_wait(r):
        cols = orecv.at[:, pl.ds(r * KR, KR)]
        pltpu.make_async_copy(cols, cols, or_.at[r]).wait()

    def project(r):
        def step(n, carry):
            cols = pl.ds(pl.multiple_of(n * 640, 128), 640)
            rows = pl.ds(pl.multiple_of(n * 640, 128), 640)
            part = nt_dot(orecv[:, r * KR : (r + 1) * KR], wt[rows, r * KR : (r + 1) * KR])
            if r == 0:
                acc[:, cols] = tok[:, cols].astype(F32) + part
            elif r < ROUNDS - 1:
                acc[:, cols] += part
            else:
                blk[:, cols] = (acc[:, cols] + part).astype(BF16)
            return carry

        lax.fori_loop(0, 5, step, 0)

    for i in range(1, NX):
        a_copy(i, x).start()
    for i in range(1, NX):
        x1_copy(i, x).start()
    qkv_start(0)
    merge_a()
    z2_start(0)
    z2_start(1)
    qkv_start(1)
    qkv_start(2)

    for n in range(8):
        emb[0, n : n + 1, :] = cap_ref[0:1, 128 * n : 128 * (n + 1)]
    own_cap = emb[0]
    norm = jnp.sqrt(jnp.sum(own_cap * own_cap, keepdims=True) + 1e-06)
    caps[z, x] = own_cap / norm

    def cap_x(i, xx):
        ref = caps.at[z, xx]
        return remote(ref, ref, cs.at[0], cr.at[i - 1], at_x(lax.rem(x + i, NX)))

    def cap_z(i, zz):
        ref = caps.at[zz]
        return remote(ref, ref, cs.at[1], cr.at[NX - 2 + i], at_z(lax.rem(z + i, NZ)))

    for i in range(1, NX):
        cap_x(i, x).start()

    z2_step(0, 1)
    z2_step(1, 1)
    merge_x()
    z1_start(0)
    z2_step(0, 2)
    z2_step(1, 2)
    z1_start(1)
    for i in range(1, NX):
        cap_x(i, lax.rem(x - i + NX, NX)).wait_recv()
    for i in range(1, NZ):
        cap_z(i, z).start()
    z2_step(0, 3)
    z2_step(1, 3)
    z2_step(0, 4)
    z2_step(1, 4)

    qkv_wait(0)
    prepare(0)
    attend(0, 8)

    z1_step(0, 1)
    z1_step(1, 1)
    x2_forward(0, 0)
    x2_forward(0, 1)
    x2_forward(0, 2)
    z1_step(0, 2)
    x2_forward(0, 3)
    x2_forward(0, 4)
    z1_step(1, 2)

    qkv_wait(1)
    prepare(1)
    attend(1, 8)

    sib_start(2)
    x2_forward(0, 5)
    x2_forward(0, 6)
    z1_step(0, 3)
    z1_step(1, 3)
    x2_forward(0, 7)
    for o in range(4):
        x2_forward(1, o)
    z1_step(0, 4)
    z1_step(1, 4)
    sib_start(0)

    qkv_wait(2)
    prepare(2)
    attend(2, 4)

    for o in range(4, 8):
        x2_forward(1, o)
    x2_near(0)
    x2_far(0)
    sib_start(1)
    x2_near(1)
    sib_start(3)
    sib_start(4)
    loads[1].wait()
    loads[2].wait()
    sib_wait(0)
    attended_wait(0)
    project(0)
    sib_wait(1)
    attended_wait(1)
    project(1)
    x2_far(1)
    sib_start(5)
    for i in range(1, NZ):
        cap_z(i, lax.rem(z - i + NZ, NZ)).wait_recv()
    for which in range(2, 6):
        sib_wait(which)
    attended_wait(2)
    project(2)
    store = pltpu.make_async_copy(blk, out_hbm, lsem.at[0])
    store.start()

    scores = nt_dot(pk_ref[...], blk[...])
    token = lax.broadcasted_iota(jnp.int32, (G, TOK), 1) + f * TOK
    live = token // TPF < valid
    masked = jnp.where(live, scores, -1e30)
    peak = jnp.max(masked, axis=1, keepdims=True)
    expo = jnp.where(live, jnp.exp(masked - peak), 0.0)
    total = jnp.sum(expo, axis=1, keepdims=True)
    e0 = expo.astype(BF16)
    rest = expo - e0.astype(F32)
    e1 = rest.astype(BF16)
    e2 = (rest - e1.astype(F32)).astype(BF16)
    w48 = jnp.dot(jnp.concatenate([e0, e1, e2], axis=0), blk[...], preferred_element_type=F32)
    w16 = w48[0:G] + w48[G : 2 * G] + w48[2 * G : 3 * G]
    mine = lax.broadcasted_iota(jnp.int32, (G, D), 1) // (D // G) == lax.broadcasted_iota(jnp.int32, (G, D), 0)

    def spread(value):
        return jnp.sum(jnp.where(mine, value, 0.0), axis=0, keepdims=True)

    msg[0:1, :] = spread(w16)
    msg[1:2, :] = spread(jnp.broadcast_to(peak, (G, D)))
    msg[2:3, :] = spread(jnp.broadcast_to(total, (G, D)))
    msg[3:8, :] = jnp.zeros((5, D), F32)
    for t in range(NF):
        pout[t, :, 400:512] = jnp.zeros((8, 112), F32)
        pout[t, :, 0:400] = msg[:, 400 * t : 400 * (t + 1)]

    def part_copy(i, src):
        t = lax.rem(f + i, NF)
        return remote(pout.at[t], parts.at[src], ms, mr.at[i - 1], {"frame": t})

    for i in range(1, NF):
        part_copy(i, f).start()
    parts[f] = pout[f]

    sent(stage_a.at[pl.ds(0, 3)], as_)
    sent(stage_x.at[pl.ds(0, 3)], x1s)
    sent(wt.at[pl.ds(0, 2800), pl.ds(0, 256)], z2s)
    sent(wt.at[pl.ds(0, 2800), pl.ds(0, 512)], z1s)
    sent(wt.at[:, pl.ds(0, 768)], x2s)
    sent(wt.at[:, pl.ds(0, 1536)], sbs)
    for r in range(ROUNDS):
        sent(qkv.at[r, :, pl.ds(0, SEQ - TOK), :], qs.at[r])
        sent(orecv.at[:, pl.ds(0, KR - HD)], os_.at[r])
    sent(caps.at[0, pl.ds(0, 3)], cs.at[0])
    sent(caps.at[pl.ds(0, 7)], cs.at[1])

    for i in range(1, NF):
        part_copy(i, lax.rem(f - i + NF, NF)).wait_recv()
    gathered = parts[...]
    peaks = gathered[:, 1, :]
    top = jnp.max(peaks, axis=0, keepdims=True)
    scale = jnp.exp(peaks - top)
    denominator = jnp.sum(gathered[:, 2, :] * scale, axis=0, keepdims=True)
    pooled = jnp.sum(gathered[:, 0, :] * scale, axis=0, keepdims=True) / denominator
    column = jnp.transpose(jnp.broadcast_to(pooled, (128, 512)))[0:400]
    for n in range(8):
        emb[0, n : n + 1, :] = jnp.sum(column * proj[:, 128 * n : 128 * (n + 1)], axis=0, keepdims=True)

    def emb_copy(i, src):
        return remote(emb.at[0], embs.at[src], es, er.at[i - 1], {"frame": lax.rem(f + i, NF)})

    for i in range(1, NF):
        emb_copy(i, f).start()
    embs[f] = emb[0]
    for i in range(1, NF):
        emb_copy(i, lax.rem(f - i + NF, NF)).wait_recv()
    raw = jnp.sum(embs[...], axis=0)
    clip = raw / jnp.sqrt(jnp.sum(raw * raw, keepdims=True) + 1e-06)

    products = jnp.sum(caps[...].reshape(NZ * NX, 8, 128) * clip[None], axis=1)
    square = jnp.concatenate([products, jnp.zeros((96, 128), F32)], axis=0)
    row = SHARP * jnp.sum(jnp.transpose(square), axis=0, keepdims=True)
    logit[z, x] = jnp.broadcast_to(row, (8, 128))

    def log_x(i, xx):
        ref = logit.at[z, xx]
        return remote(ref, ref, gs.at[0], gr.at[i - 1], at_x(lax.rem(x + i, NX)))

    def log_z(i, zz):
        ref = logit.at[zz]
        return remote(ref, ref, gs.at[1], gr.at[NX - 2 + i], at_z(lax.rem(z + i, NZ)))

    for i in range(1, NX):
        log_x(i, x).start()
    lane = lax.broadcasted_iota(jnp.int32, (1, 128), 1)
    own = jnp.where(lane < NZ * NX, row, -jnp.inf)
    own_top = jnp.max(own, axis=1, keepdims=True)
    row_lse = jnp.log(jnp.sum(jnp.exp(own - own_top), axis=1, keepdims=True)) + own_top
    for i in range(1, NX):
        log_x(i, lax.rem(x - i + NX, NX)).wait_recv()
    for i in range(1, NZ):
        log_z(i, z).start()
    sent(pout.at[pl.ds(0, 7)], ms)
    sent(embs.at[pl.ds(0, 7)], es)
    sent(logit.at[0, pl.ds(0, 3)], gs.at[0])
    store.wait()
    for i in range(1, NZ):
        log_z(i, lax.rem(z - i + NZ, NZ)).wait_recv()
    table = logit[...].reshape(NZ * NX, 8, 128)
    col_top = jnp.max(table, axis=0)
    col_lse = (jnp.log(jnp.sum(jnp.exp(table - col_top[None]), axis=0)) + col_top)[0:1, :]
    picked = jnp.where(lane == dp, 0.5 * col_lse - row, 0.0)
    value = 0.5 * row_lse + jnp.sum(picked, axis=1, keepdims=True)
    loss_ref[...] = jnp.broadcast_to(value, (1, 128))
    sent(logit.at[pl.ds(0, 7)], gs.at[1])


def local(
    queries, keys, values, tokens_in, out_weight, pool_keys, proj_weight, captions, valid_frames
):
    any_ = pl.BlockSpec(memory_space=pl.ANY)
    vmem = pl.BlockSpec(memory_space=pltpu.VMEM)
    smem = pl.BlockSpec(memory_space=pltpu.SMEM)
    dma = pltpu.SemaphoreType.DMA
    block_out, loss = pl.pallas_call(
        body,
        out_shape=(
            jax.ShapeDtypeStruct((TOK, D), BF16),
            jax.ShapeDtypeStruct((1, 128), F32),
        ),
        in_specs=[any_, any_, any_, any_, any_, vmem, any_, vmem, smem],
        out_specs=(any_, vmem),
        scratch_shapes=[
            pltpu.VMEM((TOK, D), BF16),
            pltpu.VMEM((PIECE, HEADS * HD), BF16),
            pltpu.VMEM((400, 1024), F32),
            pltpu.VMEM((NX, 112, 256), BF16),
            pltpu.VMEM((112, 512), BF16),
            pltpu.VMEM((NX, 112, 256), BF16),
            pltpu.VMEM((NX, 112, 512), BF16),
            pltpu.VMEM((416, 512), F32),
            pltpu.VMEM((D, HEADS * HD), BF16),
            pltpu.VMEM((ROUNDS, 3, SEQ, HD), BF16),
            pltpu.VMEM((SEQ, 2 * HD), BF16),
            pltpu.VMEM((SEQ, 2 * HD), BF16),
            pltpu.VMEM((ROUNDS, NF, TOK, HD), BF16),
            pltpu.VMEM((TOK, HEADS * HD), BF16),
            pltpu.VMEM((TOK, D), F32),
            pltpu.VMEM((TOK, D), BF16),
            pltpu.VMEM((8, D), F32),
            pltpu.VMEM((NF, 8, 512), F32),
            pltpu.VMEM((NF, 8, 512), F32),
            pltpu.VMEM((1, 8, 128), F32),
            pltpu.VMEM((NF, 8, 128), F32),
            pltpu.VMEM((NZ, NX, 8, 128), F32),
            pltpu.VMEM((NZ, NX, 8, 128), F32),
            dma((3,)),
            dma((ROUNDS,)), dma((ROUNDS,)),
            dma((ROUNDS,)), dma((ROUNDS,)),
            dma, dma((3,)),
            dma, dma((3,)),
            dma, dma((2, 2, 4)),
            dma, dma((2, 2, 4)),
            dma, dma((2, 2, NZ)), dma((2, NZ)),
            dma, dma((6,)),
            dma((2,)), dma((10,)),
            dma, dma((7,)),
            dma, dma((7,)),
            dma((2,)), dma((10,)),
        ],
        compiler_params=pltpu.CompilerParams(
            collective_id=0, has_side_effects=True, vmem_limit_bytes=60 * 2**20
        ),
    )(
        queries[0], keys[0], values[0], tokens_in[0], out_weight.T, pool_keys.T, proj_weight, captions, valid_frames
    )
    return block_out[None], loss[0, 0:1]


def solution(mesh):
    placed = (
        P("dp", "frame", None),
        P("dp", "frame", None),
        P("dp", "frame", None),
        P("dp", "frame", None),
        P(None, "dp"),
        P(),
        P("frame", None),
        P("dp", None),
        P("dp"),
    )
    return jax.shard_map(
        local,
        mesh=mesh,
        in_specs=placed,
        out_specs=(P("dp", "frame", None), P("dp")),
        check_vma=False,
    )
```

```python
import functools

import jax
import jax.numpy as jnp
from jax import lax
from jax.experimental import pallas as pl
from jax.experimental.pallas import tpu as pltpu
from jax.sharding import PartitionSpec as P

D = 3200
HEADS = 24
HD = 128
G = 16
TPF = 128
SEQ = 2048
TOK = 256
ROUNDS = 3
NF = 8
NZ = 8
NX = 4
KR = NF * HD
TILE_AT = (0, 2 * KR)
HALF_AT = KR
PIECE = 100
SCALE = 1.4426950408889634 / (128.0**0.5)
SHARP = 1.0 / 0.07
FAR_FIRST = (4, 3, 5, 2, 6, 1, 7)

MESH = pl.DeviceIdType.MESH
F32 = jnp.float32
BF16 = jnp.bfloat16


def nt_dot(a, b):
    return lax.dot_general(a, b, (((1,), (1,)), ((), ())), preferred_element_type=F32)


def body(
    q_hbm, k_hbm, v_hbm, tok_hbm, w_hbm, pk_hbm, proj_hbm, cap_hbm, valid_ref,
    blk, loss_ref,
    tok, wown, proj, pool, cap, own_a, own_x, stage_a, stage_x, m32, wt, qkv, k2, vext, osend, orecv, acc,
    msg, pout, parts, emb, embs, caps, logit,
    lsem, qs, qr, os_, or_, as_, ar, x1s, x1r, z1s, z1r, z2s, z2r, x2s, x2r, x2f, sbs, sbr,
    cs, cr, ms, mr, es, er, gs, gr,
):
    dp = lax.axis_index("dp")
    f = lax.axis_index("frame")
    z = dp // NX
    x = lax.rem(dp, NX)
    c = lax.rem(f, 2)
    sib = f + 1 - 2 * c
    sign = 1 - 2 * c
    valid = valid_ref[0]
    right = lax.rem(x + 1, NX)
    left = lax.rem(x + NX - 1, NX)
    across = lax.rem(x + 2, NX)

    def at_z(zz):
        return {"dp": zz * NX + x}

    def at_x(xx):
        return {"dp": z * NX + xx}

    def remote(src, dst, ssem, rsem, where):
        return pltpu.make_async_remote_copy(
            src_ref=src, dst_ref=dst, send_sem=ssem, recv_sem=rsem, device_id=where, device_id_type=MESH
        )

    def passed(ref, sem):
        pltpu.make_async_copy(ref, ref, sem).wait()

    loads = [
        pltpu.make_async_copy(w_hbm, wown, lsem.at[0]),
        pltpu.make_async_copy(tok_hbm, tok, lsem.at[1]),
        pltpu.make_async_copy(cap_hbm, cap, lsem.at[2]),
        pltpu.make_async_copy(proj_hbm, proj, lsem.at[3]),
        pltpu.make_async_copy(pk_hbm, pool, lsem.at[4]),
    ]
    for load in loads:
        load.start()

    barrier = pltpu.get_barrier_semaphore()
    for i in range(1, NF):
        pl.semaphore_signal(barrier, inc=1, device_id={"frame": lax.rem(f + i, NF)}, device_id_type=MESH)
    for i in range(1, NX):
        pl.semaphore_signal(barrier, inc=1, device_id=at_x(lax.rem(x + i, NX)), device_id_type=MESH)
    for i in range(1, NZ):
        pl.semaphore_signal(barrier, inc=1, device_id=at_z(lax.rem(z + i, NZ)), device_id_type=MESH)

    half = pl.multiple_of(c * 512, 512)
    pl.semaphore_wait(barrier, NF - 1 + NX - 1 + NZ - 1)

    def a_copy(i, src):
        to = lax.rem(x + i, NX)
        return remote(own_a.at[to], stage_a.at[src], as_, ar.at[i - 1], at_x(to))

    def x1_copy(i, src):
        return remote(own_x, stage_x.at[src], x1s, x1r.at[i - 1], at_x(lax.rem(x + i, NX)))

    def owner_lanes(tile, xx):
        return pl.ds(pl.multiple_of(TILE_AT[tile] + half + xx * 128, 128), 128)

    def half_lanes(h):
        return pl.ds(pl.multiple_of(HALF_AT + half + 256 * h, 256), 256)

    def block_rows(zb):
        return pl.ds(pl.multiple_of(400 * zb, 16), 400)

    def zmove(part, way, step):
        s = sign if way == part else -sign
        return lax.rem(z - s * step + NZ, NZ)

    def znext(part, way):
        s = sign if way == part else -sign
        return lax.rem(z + s + NZ, NZ)

    LAST = (4, 3)

    def z2_copy(tile, way, step, sem_step):
        ref = wt.at[block_rows(zmove(tile, way, step)), owner_lanes(tile, x)]
        return remote(ref, ref, z2s, z2r.at[tile, way, sem_step], at_z(znext(tile, way)))

    def z1_copy(h, way, step, sem_step):
        ref = wt.at[block_rows(zmove(h, way, step)), half_lanes(h)]
        return remote(ref, ref, z1s, z1r.at[h, way, sem_step], at_z(znext(h, way)))

    def place(tile, o):
        return zmove(tile, 0, (o + 1) // 2) if o % 2 else zmove(tile, 1, o // 2)

    def x2_copy(tile, way, o, xx):
        ref = wt.at[block_rows(place(tile, o)), owner_lanes(tile, xx)]
        return remote(ref, ref, x2s, x2r.at[tile, way, o], at_x(right if way == 0 else left))

    def x2_forward_copy(tile, way, o, xx):
        ref = wt.at[block_rows(place(tile, o)), owner_lanes(tile, xx)]
        return remote(ref, ref, x2s, x2f.at[tile, o], at_x(right if way == 0 else left))

    def x2_own(tile, o):
        x2_copy(tile, 0, o, x).start()
        x2_copy(tile, 1, o, x).start()

    def x2_forward(tile, o):
        way, xx = ((0, left), (1, right))[o % 2]
        x2_copy(tile, way, o, xx).wait_recv()
        x2_forward_copy(tile, way, o, xx).start()

    def x2_near(tile):
        for o in range(NZ):
            way, xx = ((1, right), (0, left))[o % 2]
            x2_copy(tile, way, o, xx).wait_recv()

    def x2_far(tile):
        for o in range(NZ):
            x2_forward_copy(tile, o % 2, o, across).wait_recv()

    def z2_start(tile):
        for way in range(2):
            z2_copy(tile, way, 0, 0).start()

    def z2_step(tile, step):
        for way in range(2):
            if step <= LAST[way]:
                z2_copy(tile, way, step, step - 1).wait_recv()
                if step < LAST[way]:
                    z2_copy(tile, way, step, step).start()
                x2_own(tile, 2 * step - 1 if way == 0 else 2 * step)

    def z1_start(h):
        for way in range(2):
            z1_copy(h, way, 0, 0).start()

    def z1_step(h, step):
        for way in range(2):
            if step <= LAST[way]:
                z1_copy(h, way, step, step - 1).wait_recv()
                if step < LAST[way]:
                    z1_copy(h, way, step, step).start()

    def sib_copy(which, core):
        base = core * 512
        if which == 0:
            lanes = pl.ds(pl.multiple_of(HALF_AT + base, 512), 512)
        else:
            tile, nth = divmod(which - 1, 4)
            xx = (x, left, right, across)[nth]
            lanes = pl.ds(pl.multiple_of(TILE_AT[tile] + base + xx * 128, 128), 128)
        ref = wt.at[:, lanes]
        return remote(ref, ref, sbs, sbr.at[which], {"frame": sib})

    def sib_start(which):
        sib_copy(which, c).start()

    def sib_wait(which):
        sib_copy(which, 1 - c).wait_recv()

    def merge_a():
        stage_a[x] = own_a[x]
        for i in range(1, NX):
            a_copy(i, lax.rem(x - i + NX, NX)).wait_recv()
        for i in range(NX):
            m32[PIECE * i : PIECE * i + 112, 0:256] = stage_a[i].astype(F32)
        for tile in range(2):
            wt[block_rows(z), owner_lanes(tile, x)] = m32[0:400, 128 * tile : 128 * (tile + 1)].astype(BF16)

    def merge_x():
        stage_x[x] = own_x[...]
        for i in range(1, NX):
            x1_copy(i, lax.rem(x - i + NX, NX)).wait_recv()
        for i in range(NX):
            m32[PIECE * i : PIECE * i + 112, :] = stage_x[i].astype(F32)
        wt[block_rows(z), pl.ds(pl.multiple_of(HALF_AT + half, 512), 512)] = m32[0:400, :].astype(BF16)

    def qkv_start(r):
        for i in range(1, NF):
            t = lax.rem(f + i, NF)
            cols = pl.ds(pl.multiple_of((r * NF + t) * HD, HD), HD)
            for a, ref in enumerate((k_hbm, v_hbm, q_hbm)):
                remote(
                    ref.at[:, cols],
                    qkv.at[r, a, pl.ds(pl.multiple_of(f * TOK, TOK), TOK), :],
                    qs.at[r], qr.at[r], {"frame": t},
                ).start()
        cols = pl.ds(pl.multiple_of((r * NF + f) * HD, HD), HD)
        for a, ref in enumerate((k_hbm, v_hbm, q_hbm)):
            pltpu.make_async_copy(
                ref.at[:, cols], qkv.at[r, a, pl.ds(pl.multiple_of(f * TOK, TOK), TOK), :], qr.at[r]
            ).start()

    def qkv_wait(r):
        pltpu.make_async_copy(qkv.at[r], qkv.at[r], qr.at[r]).wait()

    def prepare(r):
        for i in range(8):
            rows = slice(256 * i, 256 * (i + 1))
            live = (lax.broadcasted_iota(jnp.int32, (256, HD), 0) + 256 * i) // TPF < valid
            kk = qkv[r, 0, rows, :].astype(F32)
            first = qkv[r, 0, 0:16, :].astype(F32)[0:1, :]
            kk = jnp.where(live, kk, jnp.broadcast_to(first, (256, HD))) * SCALE
            hi = kk.astype(BF16)
            k2[rows, 0:HD] = hi
            k2[rows, HD : 2 * HD] = (kk - hi.astype(F32)).astype(BF16)
            vext[rows, 0:HD] = jnp.where(live, qkv[r, 1, rows, :].astype(F32), 0.0).astype(BF16)
            vext[rows, HD : 2 * HD] = jnp.where(live, 1.0, 0.0).astype(BF16)

    def attend(r, start, stop):
        for i in range(start, stop):
            b = lax.rem(f + 1 + i, NF)
            qq = qkv[r, 2, pl.ds(pl.multiple_of(b * TOK, TOK), TOK), :]
            scores = nt_dot(jnp.concatenate([qq, qq], axis=1), k2[...])
            peak = jnp.max(scores, axis=1, keepdims=True)
            weights = jnp.exp2(scores - peak).astype(BF16)
            both = jnp.dot(weights, vext[...], preferred_element_type=F32)
            osend[r, b] = (both[:, 0:HD] / both[:, HD : 2 * HD]).astype(BF16)

    def give_back(r, start, stop):
        group = r + start // 4
        heads = pl.ds(pl.multiple_of(r * KR + f * HD, HD), HD)
        for i in range(start, stop):
            b = lax.rem(f + 1 + i, NF)
            if i < NF - 1:
                remote(osend.at[r, b], orecv.at[:, heads], os_.at[r], or_.at[group], {"frame": b}).start()
            else:
                pltpu.make_async_copy(osend.at[r, b], orecv.at[:, heads], or_.at[group]).start()

    def attended_wait(r):
        cols = orecv.at[:, pl.ds(r * KR, KR)]
        pltpu.make_async_copy(cols, cols, or_.at[r]).wait()

    def blocks_of_columns(step):
        def one(n, carry):
            return step(pl.ds(pl.multiple_of(n * 1024, 128), 1024), carry)

        return step(pl.ds(3072, 128), lax.fori_loop(0, 3, one, jnp.zeros((G, TOK), F32)))

    def project(r):
        def step(cols, carry):
            part = nt_dot(orecv[:, r * KR : (r + 1) * KR], wt[cols, r * KR : (r + 1) * KR])
            if r == 0:
                acc[:, cols] = tok[:, cols].astype(F32) + part
            else:
                acc[:, cols] += part
            return carry

        blocks_of_columns(step)

    def project_last(group):
        cols = orecv.at[:, pl.ds(0, 4 * HD)]
        pltpu.make_async_copy(cols, cols, or_.at[2 + group]).wait()
        lanes = []
        for i in range(1, 5):
            source = lax.rem(f - i - 4 * group + 2 * NF, NF)
            lanes.append(pl.ds(pl.multiple_of(2 * KR + source * HD, HD), HD))
        rows = jnp.concatenate([orecv[:, ln] for ln in lanes], axis=1)

        def step(cols, carry):
            part = nt_dot(rows, jnp.concatenate([wt[cols, ln] for ln in lanes], axis=1))
            if group == 0:
                acc[:, cols] += part
                return carry
            block = (acc[:, cols] + part).astype(BF16)
            blk[:, cols] = block
            return carry + nt_dot(pool[:, cols], block)

        return blocks_of_columns(step)

    qkv_start(0)

    loads[0].wait()
    for to in range(NX):
        for tile in range(2):
            lanes = pl.ds(pl.multiple_of(TILE_AT[tile] + half + to * 128, 128), 128)
            own_a[to, 0:PIECE, 128 * tile : 128 * (tile + 1)] = wown[:, lanes]
    own_x[0:PIECE, :] = wown[:, pl.ds(pl.multiple_of(HALF_AT + half, 512), 512)]
    for to in range(NX):
        own_a[to, 96:112, :] = jnp.concatenate([own_a[to, 96:112, :][0:4], jnp.zeros((12, 256), BF16)], axis=0)
    own_x[96:112, :] = jnp.concatenate([own_x[96:112, :][0:4], jnp.zeros((12, 512), BF16)], axis=0)
    for i in range(1, NX):
        a_copy(i, x).start()
    merge_a()
    z2_start(0)
    z2_start(1)
    for i in range(1, NX):
        x1_copy(i, x).start()
    x2_own(0, 0)
    x2_own(1, 0)
    qkv_start(1)
    qkv_start(2)

    loads[2].wait()
    for n in range(8):
        emb[0, n : n + 1, :] = cap[0:1, 128 * n : 128 * (n + 1)]
    own_cap = emb[0]
    norm = jnp.sqrt(jnp.sum(own_cap * own_cap, keepdims=True) + 1e-06)
    caps[z, x] = own_cap / norm

    def cap_x(i, xx):
        ref = caps.at[z, xx]
        return remote(ref, ref, cs.at[0], cr.at[i - 1], at_x(lax.rem(x + i, NX)))

    def cap_z(i, zz):
        ref = caps.at[zz]
        return remote(ref, ref, cs.at[1], cr.at[NX - 2 + i], at_z(lax.rem(z + i, NZ)))

    for i in range(1, NX):
        cap_x(i, x).start()

    z2_step(0, 1)
    z2_step(1, 1)
    z2_step(0, 2)
    z2_step(1, 2)
    merge_x()
    z1_start(0)
    z2_step(0, 3)
    z2_step(1, 3)
    z1_start(1)
    for i in range(1, NX):
        cap_x(i, lax.rem(x - i + NX, NX)).wait_recv()
    for i in range(1, NZ):
        cap_z(i, z).start()

    qkv_wait(0)
    prepare(0)
    attend(0, 0, 2)
    z2_step(0, 4)
    z2_step(1, 4)
    z1_step(0, 1)
    attend(0, 2, 6)
    z1_step(1, 1)
    attend(0, 6, 8)
    for o in range(0, 3):
        x2_forward(0, o)
    z1_step(0, 2)
    for o in range(3, 6):
        x2_forward(0, o)

    qkv_wait(1)
    prepare(1)
    attend(1, 0, 2)
    z1_step(1, 2)
    sib_start(1)
    sib_start(5)
    attend(1, 2, 5)
    z1_step(0, 3)
    x2_forward(0, 6)
    x2_forward(0, 7)
    x2_near(0)
    sib_start(2)
    sib_start(3)
    for o in range(0, 4):
        x2_forward(1, o)
    give_back(0, 0, 8)
    attend(1, 5, 8)
    give_back(1, 0, 8)
    z1_step(1, 3)
    for o in range(4, 8):
        x2_forward(1, o)
    x2_near(1)
    sib_start(6)
    sib_start(7)

    qkv_wait(2)
    prepare(2)
    attend(2, 0, 4)
    give_back(2, 0, 4)
    x2_far(0)
    sib_start(4)
    z1_step(0, 4)
    z1_step(1, 4)
    sib_start(0)
    attend(2, 4, 8)
    give_back(2, 4, 8)

    loads[1].wait()
    loads[3].wait()
    loads[4].wait()
    for which in range(1, 5):
        sib_wait(which)
    attended_wait(0)
    project(0)
    x2_far(1)
    sib_start(8)
    sib_wait(0)
    attended_wait(1)
    project(1)
    for i in range(1, NZ):
        cap_z(i, lax.rem(z - i + NZ, NZ)).wait_recv()
    for which in range(5, 9):
        sib_wait(which)
    project_last(0)
    scores = project_last(1)

    token = lax.broadcasted_iota(jnp.int32, (G, TOK), 1) + f * TOK
    live = token // TPF < valid
    masked = jnp.where(live, scores, -1e30)
    peak = jnp.max(masked, axis=1, keepdims=True)
    expo = jnp.where(live, jnp.exp(masked - peak), 0.0)
    total = jnp.sum(expo, axis=1, keepdims=True)
    e0 = expo.astype(BF16)
    rest = expo - e0.astype(F32)
    e1 = rest.astype(BF16)
    e2 = (rest - e1.astype(F32)).astype(BF16)
    w48 = jnp.dot(jnp.concatenate([e0, e1, e2], axis=0), blk[...], preferred_element_type=F32)
    w16 = w48[0:G] + w48[G : 2 * G] + w48[2 * G : 3 * G]
    mine = lax.broadcasted_iota(jnp.int32, (G, D), 1) // (D // G) == lax.broadcasted_iota(jnp.int32, (G, D), 0)

    msg[...] = jnp.sum(jnp.where(mine, w16, 0.0), axis=0, keepdims=True)
    stats = jnp.concatenate([peak, total], axis=1)
    for t in range(NF):
        pout[t, :, 0:400] = msg[:, 400 * t : 400 * (t + 1)]
        pout[t, :, 400:402] = stats[2 * t : 2 * t + 1, :]
        pout[t, :, 402:404] = stats[2 * t + 1 : 2 * t + 2, :]

    def part_copy(i, src):
        t = lax.rem(f + i, NF)
        return remote(pout.at[t], parts.at[src], ms, mr, {"frame": t})

    for i in FAR_FIRST:
        part_copy(i, f).start()
    parts[f] = pout[f]

    passed(stage_a.at[pl.ds(0, 3)], as_)
    passed(stage_x.at[pl.ds(0, 3)], x1s)
    passed(wt.at[pl.ds(0, 2800), pl.ds(0, 256)], z2s)
    passed(wt.at[pl.ds(0, 2800), pl.ds(0, 512)], z1s)
    passed(wt.at[:, pl.ds(0, 768)], x2s)
    passed(wt.at[:, pl.ds(0, 1536)], sbs)
    for r in range(ROUNDS):
        passed(qkv.at[r, :, pl.ds(0, SEQ - TOK), :], qs.at[r])
        passed(orecv.at[:, pl.ds(0, KR - HD)], os_.at[r])
    passed(caps.at[0, pl.ds(0, 3)], cs.at[0])
    passed(caps.at[pl.ds(0, 7)], cs.at[1])

    passed(parts.at[pl.ds(0, NF - 1)], mr)
    gathered = parts[...].reshape(NF, 512)
    first = lax.broadcasted_iota(jnp.int32, (NF, 512), 1) < D // G
    peaks = jnp.where(first, gathered[:, 400:401], gathered[:, 402:403])
    totals = jnp.where(first, gathered[:, 401:402], gathered[:, 403:404])
    top = jnp.max(peaks, axis=0, keepdims=True)
    scale = jnp.exp(peaks - top)
    denominator = jnp.sum(totals * scale, axis=0, keepdims=True)
    pooled = jnp.sum(gathered * scale, axis=0, keepdims=True) / denominator
    column = jnp.transpose(jnp.broadcast_to(pooled, (128, 512)))[0:400]
    for n in range(8):
        emb[0, n : n + 1, :] = jnp.sum(column * proj[:, 128 * n : 128 * (n + 1)], axis=0, keepdims=True)

    def emb_copy(i, src):
        return remote(emb.at[0], embs.at[src], es, er, {"frame": lax.rem(f + i, NF)})

    for i in FAR_FIRST:
        emb_copy(i, f).start()
    embs[f] = emb[0]
    passed(embs.at[pl.ds(0, NF - 1)], er)
    raw = jnp.sum(embs[...], axis=0)
    clip = raw / jnp.sqrt(jnp.sum(raw * raw, keepdims=True) + 1e-06)

    products = jnp.sum(caps[...].reshape(NZ * NX, 8, 128) * clip[None], axis=1)
    square = jnp.concatenate([products, jnp.zeros((96, 128), F32)], axis=0)
    row = SHARP * jnp.sum(jnp.transpose(square), axis=0, keepdims=True)
    logit[dp] = row

    def log_copy(i, src):
        ref = logit.at[src]
        to = lax.rem(dp + i, NZ * NX)
        return remote(ref, ref, gs, gr, {"dp": to})

    def log_start(i, carry):
        log_copy(1 + lax.rem(i + 11, NZ * NX - 1), dp).start()
        return carry

    lax.fori_loop(0, NZ * NX - 1, log_start, 0)
    lane = lax.broadcasted_iota(jnp.int32, (1, 128), 1)
    own = jnp.where(lane < NZ * NX, row, -jnp.inf)
    own_top = jnp.max(own, axis=1, keepdims=True)
    row_lse = jnp.log(jnp.sum(jnp.exp(own - own_top), axis=1, keepdims=True)) + own_top
    passed(pout.at[pl.ds(0, 7)], ms)
    passed(embs.at[pl.ds(0, 7)], es)

    passed(logit.at[pl.ds(0, NZ * NX - 1)], gr)
    table = logit[...].reshape(NZ * NX, 128)
    col_top = jnp.max(table, axis=0, keepdims=True)
    col_lse = jnp.log(jnp.sum(jnp.exp(table - col_top), axis=0, keepdims=True)) + col_top
    picked = jnp.where(lane == dp, 0.5 * col_lse - row, 0.0)
    value = 0.5 * row_lse + jnp.sum(picked, axis=1, keepdims=True)
    loss_ref[...] = jnp.broadcast_to(value, (1, 128))
    passed(logit.at[pl.ds(0, NZ * NX - 1)], gs)


def local(
    queries, keys, values, tokens_in, out_weight, pool_keys, proj_weight, captions, valid_frames
):
    any_ = pl.BlockSpec(memory_space=pl.ANY)
    vmem = pl.BlockSpec(memory_space=pltpu.VMEM)
    smem = pl.BlockSpec(memory_space=pltpu.SMEM)
    dma = pltpu.SemaphoreType.DMA
    block_out, loss = pl.pallas_call(
        body,
        out_shape=(
            pltpu.VMEM((TOK, D), BF16),
            jax.ShapeDtypeStruct((1, 128), F32),
        ),
        in_specs=[any_, any_, any_, any_, any_, any_, any_, any_, smem],
        out_specs=(vmem, vmem),
        scratch_shapes=[
            pltpu.VMEM((TOK, D), BF16),
            pltpu.VMEM((PIECE, HEADS * HD), BF16),
            pltpu.VMEM((400, 1024), F32),
            pltpu.VMEM((G, D), BF16),
            pltpu.VMEM((1, 1024), F32),
            pltpu.VMEM((NX, 112, 256), BF16),
            pltpu.VMEM((112, 512), BF16),
            pltpu.VMEM((NX, 112, 256), BF16),
            pltpu.VMEM((NX, 112, 512), BF16),
            pltpu.VMEM((416, 512), F32),
            pltpu.VMEM((D, HEADS * HD), BF16),
            pltpu.VMEM((ROUNDS, 3, SEQ, HD), BF16),
            pltpu.VMEM((SEQ, 2 * HD), BF16),
            pltpu.VMEM((SEQ, 2 * HD), BF16),
            pltpu.VMEM((ROUNDS, NF, TOK, HD), BF16),
            pltpu.VMEM((TOK, HEADS * HD), BF16),
            pltpu.VMEM((TOK, D), F32),
            pltpu.VMEM((1, D), F32),
            pltpu.VMEM((NF, 1, 512), F32),
            pltpu.VMEM((NF, 1, 512), F32),
            pltpu.VMEM((1, 8, 128), F32),
            pltpu.VMEM((NF, 8, 128), F32),
            pltpu.VMEM((NZ, NX, 8, 128), F32),
            pltpu.VMEM((NZ * NX, 1, 128), F32),
            dma((5,)),
            dma((ROUNDS,)), dma((ROUNDS,)),
            dma((ROUNDS,)), dma((ROUNDS + 1,)),
            dma, dma((3,)),
            dma, dma((3,)),
            dma, dma((2, 2, 4)),
            dma, dma((2, 2, 4)),
            dma, dma((2, 2, NZ)), dma((2, NZ)),
            dma, dma((9,)),
            dma((2,)), dma((10,)),
            dma, dma,
            dma, dma,
            dma, dma,
        ],
        compiler_params=pltpu.CompilerParams(
            collective_id=0, has_side_effects=True, vmem_limit_bytes=60 * 2**20
        ),
    )(
        queries[0], keys[0], values[0], tokens_in[0], out_weight.T, pool_keys.T, proj_weight, captions, valid_frames
    )
    return block_out[None], loss[0, 0:1]


def solution(mesh):
    placed = (
        P("dp", "frame", None),
        P("dp", "frame", None),
        P("dp", "frame", None),
        P("dp", "frame", None),
        P(None, "dp"),
        P(),
        P("frame", None),
        P("dp", None),
        P("dp"),
    )
    return jax.shard_map(
        local,
        mesh=mesh,
        in_specs=placed,
        out_specs=(P("dp", "frame", None), P("dp")),
        check_vma=False,
    )
```

```python
import functools

import jax
import jax.numpy as jnp
from jax import lax
from jax.experimental import pallas as pl
from jax.experimental.pallas import tpu as pltpu
from jax.sharding import PartitionSpec as P

D = 3200
HEADS = 24
HD = 128
G = 16
TPF = 128
SEQ = 2048
TOK = 256
ROUNDS = 3
NF = 8
NZ = 8
NX = 4
KR = NF * HD
TILE_AT = (0, 2 * KR)
HALF_AT = KR
PIECE = 100
SCALE = 1.4426950408889634 / (128.0**0.5)
SHARP = 1.0 / 0.07
FAR_FIRST = (4, 3, 5, 2, 6, 1, 7)

MESH = pl.DeviceIdType.MESH
F32 = jnp.float32
BF16 = jnp.bfloat16


def nt_dot(a, b):
    return lax.dot_general(a, b, (((1,), (1,)), ((), ())), preferred_element_type=F32)


def body(
    q_hbm, k_hbm, v_hbm, tok_hbm, w_hbm, pk_hbm, proj_hbm, cap_hbm, valid_hbm,
    out_ref, loss_out,
    tok, wown, proj, pool, cap, count, blk, loss, own_a, own_x, stage_a, stage_x, m32, wt, qkv, k2, vext, osend, orecv, acc,
    msg, pout, parts, emb, embs, caps, logit,
    lsem, qs, qr, os_, or_, as_, ar, x1s, x1r, z1s, z1r, z2s, z2r, x2s, x2r, x2f, sbs, sbr,
    cs, cr, ms, mr, es, er, gs, gr,
):
    dp = lax.axis_index("dp")
    f = lax.axis_index("frame")
    z = dp // NX
    x = lax.rem(dp, NX)
    c = lax.rem(f, 2)
    sib = f + 1 - 2 * c
    sign = 1 - 2 * c
    right = lax.rem(x + 1, NX)
    left = lax.rem(x + NX - 1, NX)
    across = lax.rem(x + 2, NX)

    def at_z(zz):
        return {"dp": zz * NX + x}

    def at_x(xx):
        return {"dp": z * NX + xx}

    def remote(src, dst, ssem, rsem, where):
        return pltpu.make_async_remote_copy(
            src_ref=src, dst_ref=dst, send_sem=ssem, recv_sem=rsem, device_id=where, device_id_type=MESH
        )

    def passed(ref, sem):
        pltpu.make_async_copy(ref, ref, sem).wait()

    loads = [
        pltpu.make_async_copy(w_hbm, wown, lsem.at[0]),
        pltpu.make_async_copy(tok_hbm, tok, lsem.at[1]),
        pltpu.make_async_copy(cap_hbm, cap, lsem.at[2]),
        pltpu.make_async_copy(proj_hbm, proj, lsem.at[3]),
        pltpu.make_async_copy(pk_hbm, pool, lsem.at[4]),
        pltpu.make_async_copy(valid_hbm, count, lsem.at[5]),
    ]
    for load in loads:
        load.start()

    barrier = pltpu.get_barrier_semaphore()
    for i in range(1, NF):
        pl.semaphore_signal(barrier, inc=1, device_id={"frame": lax.rem(f + i, NF)}, device_id_type=MESH)
    for i in range(1, NX):
        pl.semaphore_signal(barrier, inc=1, device_id=at_x(lax.rem(x + i, NX)), device_id_type=MESH)
    for i in range(1, NZ):
        pl.semaphore_signal(barrier, inc=1, device_id=at_z(lax.rem(z + i, NZ)), device_id_type=MESH)

    half = pl.multiple_of(c * 512, 512)
    pl.semaphore_wait(barrier, NF - 1 + NX - 1 + NZ - 1)

    def a_copy(i, src):
        to = lax.rem(x + i, NX)
        return remote(own_a.at[to], stage_a.at[src], as_, ar.at[i - 1], at_x(to))

    def x1_copy(i, src):
        return remote(own_x, stage_x.at[src], x1s, x1r.at[i - 1], at_x(lax.rem(x + i, NX)))

    def owner_lanes(tile, xx):
        return pl.ds(pl.multiple_of(TILE_AT[tile] + half + xx * 128, 128), 128)

    def half_lanes(h):
        return pl.ds(pl.multiple_of(HALF_AT + half + 256 * h, 256), 256)

    def block_rows(zb):
        return pl.ds(pl.multiple_of(400 * zb, 16), 400)

    def zmove(part, way, step):
        s = sign if way == part else -sign
        return lax.rem(z - s * step + NZ, NZ)

    def znext(part, way):
        s = sign if way == part else -sign
        return lax.rem(z + s + NZ, NZ)

    LAST = (4, 3)

    def z2_copy(tile, way, step, sem_step):
        ref = wt.at[block_rows(zmove(tile, way, step)), owner_lanes(tile, x)]
        return remote(ref, ref, z2s, z2r.at[tile, way, sem_step], at_z(znext(tile, way)))

    def z1_copy(h, way, step, sem_step):
        ref = wt.at[block_rows(zmove(h, way, step)), half_lanes(h)]
        return remote(ref, ref, z1s, z1r.at[h, way, sem_step], at_z(znext(h, way)))

    def place(tile, o):
        return zmove(tile, 0, (o + 1) // 2) if o % 2 else zmove(tile, 1, o // 2)

    def x2_copy(tile, way, o, xx):
        ref = wt.at[block_rows(place(tile, o)), owner_lanes(tile, xx)]
        return remote(ref, ref, x2s, x2r.at[tile, way, o], at_x(right if way == 0 else left))

    def x2_forward_copy(tile, way, o, xx):
        ref = wt.at[block_rows(place(tile, o)), owner_lanes(tile, xx)]
        return remote(ref, ref, x2s, x2f.at[tile, o], at_x(right if way == 0 else left))

    def x2_own(tile, o):
        x2_copy(tile, 0, o, x).start()
        x2_copy(tile, 1, o, x).start()

    def x2_forward(tile, o):
        way, xx = ((0, left), (1, right))[o % 2]
        x2_copy(tile, way, o, xx).wait_recv()
        x2_forward_copy(tile, way, o, xx).start()

    def x2_near(tile):
        for o in range(NZ):
            way, xx = ((1, right), (0, left))[o % 2]
            x2_copy(tile, way, o, xx).wait_recv()

    def x2_far(tile):
        for o in range(NZ):
            x2_forward_copy(tile, o % 2, o, across).wait_recv()

    def z2_start(tile):
        for way in range(2):
            z2_copy(tile, way, 0, 0).start()

    def z2_step(tile, step):
        for way in range(2):
            if step <= LAST[way]:
                z2_copy(tile, way, step, step - 1).wait_recv()
                if step < LAST[way]:
                    z2_copy(tile, way, step, step).start()
                x2_own(tile, 2 * step - 1 if way == 0 else 2 * step)

    def z1_start(h):
        for way in range(2):
            z1_copy(h, way, 0, 0).start()

    def z1_step(h, step):
        for way in range(2):
            if step <= LAST[way]:
                z1_copy(h, way, step, step - 1).wait_recv()
                if step < LAST[way]:
                    z1_copy(h, way, step, step).start()

    def sib_copy(which, core):
        base = core * 512
        if which == 0:
            lanes = pl.ds(pl.multiple_of(HALF_AT + base, 512), 512)
        else:
            tile, nth = divmod(which - 1, 4)
            xx = (x, left, right, across)[nth]
            lanes = pl.ds(pl.multiple_of(TILE_AT[tile] + base + xx * 128, 128), 128)
        ref = wt.at[:, lanes]
        return remote(ref, ref, sbs, sbr.at[which], {"frame": sib})

    def sib_start(which):
        sib_copy(which, c).start()

    def sib_wait(which):
        sib_copy(which, 1 - c).wait_recv()

    def merge_a():
        stage_a[x] = own_a[x]
        for i in range(1, NX):
            a_copy(i, lax.rem(x - i + NX, NX)).wait_recv()
        for i in range(NX):
            m32[PIECE * i : PIECE * i + 112, 0:256] = stage_a[i].astype(F32)
        for tile in range(2):
            wt[block_rows(z), owner_lanes(tile, x)] = m32[0:400, 128 * tile : 128 * (tile + 1)].astype(BF16)

    def merge_x():
        stage_x[x] = own_x[...]
        for i in range(1, NX):
            x1_copy(i, lax.rem(x - i + NX, NX)).wait_recv()
        for i in range(NX):
            m32[PIECE * i : PIECE * i + 112, :] = stage_x[i].astype(F32)
        wt[block_rows(z), pl.ds(pl.multiple_of(HALF_AT + half, 512), 512)] = m32[0:400, :].astype(BF16)

    def qkv_start(r):
        for i in range(1, NF):
            t = lax.rem(f + i, NF)
            cols = pl.ds(pl.multiple_of((r * NF + t) * HD, HD), HD)
            for a, ref in enumerate((k_hbm, v_hbm, q_hbm)):
                remote(
                    ref.at[:, cols],
                    qkv.at[r, a, pl.ds(pl.multiple_of(f * TOK, TOK), TOK), :],
                    qs.at[r], qr.at[r], {"frame": t},
                ).start()
        cols = pl.ds(pl.multiple_of((r * NF + f) * HD, HD), HD)
        for a, ref in enumerate((k_hbm, v_hbm, q_hbm)):
            pltpu.make_async_copy(
                ref.at[:, cols], qkv.at[r, a, pl.ds(pl.multiple_of(f * TOK, TOK), TOK), :], qr.at[r]
            ).start()

    def qkv_wait(r):
        pltpu.make_async_copy(qkv.at[r], qkv.at[r], qr.at[r]).wait()

    def prepare(r, valid):
        for i in range(8):
            rows = slice(256 * i, 256 * (i + 1))
            live = (lax.broadcasted_iota(jnp.int32, (256, HD), 0) + 256 * i) // TPF < valid
            kk = qkv[r, 0, rows, :].astype(F32)
            first = qkv[r, 0, 0:16, :].astype(F32)[0:1, :]
            kk = jnp.where(live, kk, jnp.broadcast_to(first, (256, HD))) * SCALE
            hi = kk.astype(BF16)
            k2[rows, 0:HD] = hi
            k2[rows, HD : 2 * HD] = (kk - hi.astype(F32)).astype(BF16)
            vext[rows, 0:HD] = jnp.where(live, qkv[r, 1, rows, :].astype(F32), 0.0).astype(BF16)
            vext[rows, HD : 2 * HD] = jnp.where(live, 1.0, 0.0).astype(BF16)

    def attend(r, start, stop):
        for i in range(start, stop):
            b = lax.rem(f + 1 + i, NF)
            qq = qkv[r, 2, pl.ds(pl.multiple_of(b * TOK, TOK), TOK), :]
            scores = nt_dot(jnp.concatenate([qq, qq], axis=1), k2[...])
            peak = jnp.max(scores, axis=1, keepdims=True)
            weights = jnp.exp2(scores - peak).astype(BF16)
            both = jnp.dot(weights, vext[...], preferred_element_type=F32)
            osend[r, b] = (both[:, 0:HD] / both[:, HD : 2 * HD]).astype(BF16)

    def give_back(r, start, stop):
        group = r + start // 4
        heads = pl.ds(pl.multiple_of(r * KR + f * HD, HD), HD)
        for i in range(start, stop):
            b = lax.rem(f + 1 + i, NF)
            if i < NF - 1:
                remote(osend.at[r, b], orecv.at[:, heads], os_.at[r], or_.at[group], {"frame": b}).start()
            else:
                pltpu.make_async_copy(osend.at[r, b], orecv.at[:, heads], or_.at[group]).start()

    def attended_wait(r):
        cols = orecv.at[:, pl.ds(r * KR, KR)]
        pltpu.make_async_copy(cols, cols, or_.at[r]).wait()

    def blocks_of_columns(step, unroll):
        def one(n, carry):
            return step(pl.ds(pl.multiple_of(n * 1024, 128), 1024), carry)

        return step(pl.ds(3072, 128), lax.fori_loop(0, 3, one, jnp.zeros((G, TOK), F32), unroll=unroll))

    def project(r):
        def step(cols, carry):
            part = nt_dot(orecv[:, r * KR : (r + 1) * KR], wt[cols, r * KR : (r + 1) * KR])
            if r == 0:
                acc[:, cols] = tok[:, cols].astype(F32) + part
            else:
                acc[:, cols] += part
            return carry

        blocks_of_columns(step, False)

    def project_last(group):
        cols = orecv.at[:, pl.ds(0, 4 * HD)]
        pltpu.make_async_copy(cols, cols, or_.at[2 + group]).wait()
        lanes = []
        for i in range(1, 5):
            source = lax.rem(f - i - 4 * group + 2 * NF, NF)
            lanes.append(pl.ds(pl.multiple_of(2 * KR + source * HD, HD), HD))
        rows = jnp.concatenate([orecv[:, ln] for ln in lanes], axis=1)

        def step(cols, carry):
            part = nt_dot(rows, jnp.concatenate([wt[cols, ln] for ln in lanes], axis=1))
            if group == 0:
                acc[:, cols] += part
                return carry
            block = (acc[:, cols] + part).astype(BF16)
            blk[:, cols] = block
            return carry + nt_dot(pool[:, cols], block)

        return blocks_of_columns(step, True)

    qkv_start(0)

    loads[0].wait()
    for to in range(NX):
        for tile in range(2):
            lanes = pl.ds(pl.multiple_of(TILE_AT[tile] + half + to * 128, 128), 128)
            own_a[to, 0:PIECE, 128 * tile : 128 * (tile + 1)] = wown[:, lanes]
    own_x[0:PIECE, :] = wown[:, pl.ds(pl.multiple_of(HALF_AT + half, 512), 512)]
    for to in range(NX):
        own_a[to, 96:112, :] = jnp.concatenate([own_a[to, 96:112, :][0:4], jnp.zeros((12, 256), BF16)], axis=0)
    own_x[96:112, :] = jnp.concatenate([own_x[96:112, :][0:4], jnp.zeros((12, 512), BF16)], axis=0)
    for i in range(1, NX):
        a_copy(i, x).start()
    merge_a()
    z2_start(0)
    z2_start(1)
    for i in range(1, NX):
        x1_copy(i, x).start()
    x2_own(0, 0)
    x2_own(1, 0)
    qkv_start(1)
    qkv_start(2)

    loads[2].wait()
    loads[5].wait()
    valid = count[...]
    for n in range(8):
        emb[0, n : n + 1, :] = cap[0:1, 128 * n : 128 * (n + 1)]
    own_cap = emb[0]
    norm = jnp.sqrt(jnp.sum(own_cap * own_cap, keepdims=True) + 1e-06)
    caps[z, x] = own_cap / norm

    def cap_x(i, xx):
        ref = caps.at[z, xx]
        return remote(ref, ref, cs.at[0], cr.at[i - 1], at_x(lax.rem(x + i, NX)))

    def cap_z(i, zz):
        ref = caps.at[zz]
        return remote(ref, ref, cs.at[1], cr.at[NX - 2 + i], at_z(lax.rem(z + i, NZ)))

    for i in range(1, NX):
        cap_x(i, x).start()

    z2_step(0, 1)
    z2_step(1, 1)
    z2_step(0, 2)
    z2_step(1, 2)
    merge_x()
    z1_start(0)
    z2_step(0, 3)
    z2_step(1, 3)
    z1_start(1)
    for i in range(1, NX):
        cap_x(i, lax.rem(x - i + NX, NX)).wait_recv()
    for i in range(1, NZ):
        cap_z(i, z).start()

    qkv_wait(0)
    prepare(0, valid)
    attend(0, 0, 2)
    z2_step(0, 4)
    z2_step(1, 4)
    z1_step(0, 1)
    attend(0, 2, 6)
    z1_step(1, 1)
    attend(0, 6, 8)
    for o in range(0, 3):
        x2_forward(0, o)
    z1_step(0, 2)
    for o in range(3, 6):
        x2_forward(0, o)

    qkv_wait(1)
    prepare(1, valid)
    attend(1, 0, 2)
    z1_step(1, 2)
    sib_start(1)
    sib_start(5)
    attend(1, 2, 5)
    z1_step(0, 3)
    x2_forward(0, 6)
    x2_forward(0, 7)
    x2_near(0)
    sib_start(2)
    sib_start(3)
    for o in range(0, 4):
        x2_forward(1, o)
    give_back(0, 0, 8)
    attend(1, 5, 8)
    give_back(1, 0, 8)
    z1_step(1, 3)
    for o in range(4, 8):
        x2_forward(1, o)
    x2_near(1)
    sib_start(6)
    sib_start(7)

    qkv_wait(2)
    prepare(2, valid)
    attend(2, 0, 4)
    give_back(2, 0, 4)
    x2_far(0)
    sib_start(4)
    z1_step(0, 4)
    z1_step(1, 4)
    sib_start(0)
    attend(2, 4, 8)
    give_back(2, 4, 8)

    loads[1].wait()
    loads[3].wait()
    loads[4].wait()
    for which in range(1, 5):
        sib_wait(which)
    attended_wait(0)
    project(0)
    x2_far(1)
    sib_start(8)
    sib_wait(0)
    attended_wait(1)
    project(1)
    for i in range(1, NZ):
        cap_z(i, lax.rem(z - i + NZ, NZ)).wait_recv()
    for which in range(5, 9):
        sib_wait(which)
    project_last(0)
    scores = project_last(1)

    token = lax.broadcasted_iota(jnp.int32, (G, TOK), 1) + f * TOK
    live = token // TPF < valid
    masked = jnp.where(live, scores, -1e30)
    peak = jnp.max(masked, axis=1, keepdims=True)
    expo = jnp.where(live, jnp.exp(masked - peak), 0.0)
    total = jnp.sum(expo, axis=1, keepdims=True)
    e0 = expo.astype(BF16)
    rest = expo - e0.astype(F32)
    e1 = rest.astype(BF16)
    e2 = (rest - e1.astype(F32)).astype(BF16)
    w48 = jnp.dot(jnp.concatenate([e0, e1, e2], axis=0), blk[...], preferred_element_type=F32)
    w16 = w48[0:G] + w48[G : 2 * G] + w48[2 * G : 3 * G]
    mine = lax.broadcasted_iota(jnp.int32, (G, D), 1) // (D // G) == lax.broadcasted_iota(jnp.int32, (G, D), 0)

    msg[...] = jnp.sum(jnp.where(mine, w16, 0.0), axis=0, keepdims=True)
    stats = jnp.concatenate([peak, total], axis=1)
    for t in range(NF):
        pout[t, :, 0:400] = msg[:, 400 * t : 400 * (t + 1)]
        pout[t, :, 400:402] = stats[2 * t : 2 * t + 1, :]
        pout[t, :, 402:404] = stats[2 * t + 1 : 2 * t + 2, :]

    def part_copy(i, src):
        t = lax.rem(f + i, NF)
        return remote(pout.at[t], parts.at[src], ms, mr, {"frame": t})

    for i in FAR_FIRST:
        part_copy(i, f).start()
    store = pltpu.make_async_copy(blk, out_ref, lsem.at[6])
    store.start()
    parts[f] = pout[f]

    passed(stage_a.at[pl.ds(0, 3)], as_)
    passed(stage_x.at[pl.ds(0, 3)], x1s)
    passed(wt.at[pl.ds(0, 2800), pl.ds(0, 256)], z2s)
    passed(wt.at[pl.ds(0, 2800), pl.ds(0, 512)], z1s)
    passed(wt.at[:, pl.ds(0, 768)], x2s)
    passed(wt.at[:, pl.ds(0, 1536)], sbs)
    for r in range(ROUNDS):
        passed(qkv.at[r, :, pl.ds(0, SEQ - TOK), :], qs.at[r])
        passed(orecv.at[:, pl.ds(0, KR - HD)], os_.at[r])
    passed(caps.at[0, pl.ds(0, 3)], cs.at[0])
    passed(caps.at[pl.ds(0, 7)], cs.at[1])

    passed(parts.at[pl.ds(0, NF - 1)], mr)
    gathered = parts[...].reshape(NF, 512)
    first = lax.broadcasted_iota(jnp.int32, (NF, 512), 1) < D // G
    peaks = jnp.where(first, gathered[:, 400:401], gathered[:, 402:403])
    totals = jnp.where(first, gathered[:, 401:402], gathered[:, 403:404])
    top = jnp.max(peaks, axis=0, keepdims=True)
    scale = jnp.exp(peaks - top)
    denominator = jnp.sum(totals * scale, axis=0, keepdims=True)
    pooled = jnp.sum(gathered * scale, axis=0, keepdims=True) / denominator
    column = jnp.transpose(jnp.broadcast_to(pooled, (128, 512)))[0:400]
    for n in range(8):
        emb[0, n : n + 1, :] = jnp.sum(column * proj[:, 128 * n : 128 * (n + 1)], axis=0, keepdims=True)

    def emb_copy(i, src):
        return remote(emb.at[0], embs.at[src], es, er, {"frame": lax.rem(f + i, NF)})

    for i in FAR_FIRST:
        emb_copy(i, f).start()
    embs[f] = emb[0]
    passed(embs.at[pl.ds(0, NF - 1)], er)
    raw = jnp.sum(embs[...], axis=0)
    clip = raw / jnp.sqrt(jnp.sum(raw * raw, keepdims=True) + 1e-06)

    products = jnp.sum(caps[...].reshape(NZ * NX, 8, 128) * clip[None], axis=1)
    square = jnp.concatenate([products, jnp.zeros((96, 128), F32)], axis=0)
    row = SHARP * jnp.sum(jnp.transpose(square), axis=0, keepdims=True)
    logit[dp] = row

    def log_copy(i, src):
        ref = logit.at[src]
        to = lax.rem(dp + i, NZ * NX)
        return remote(ref, ref, gs, gr, {"dp": to})

    for i in range(NZ * NX - 1):
        log_copy(1 + (i + 11) % (NZ * NX - 1), dp).start()
    lane = lax.broadcasted_iota(jnp.int32, (1, 128), 1)
    own = jnp.where(lane < NZ * NX, row, -jnp.inf)
    own_top = jnp.max(own, axis=1, keepdims=True)
    row_lse = jnp.log(jnp.sum(jnp.exp(own - own_top), axis=1, keepdims=True)) + own_top
    passed(pout.at[pl.ds(0, 7)], ms)
    passed(embs.at[pl.ds(0, 7)], es)

    store.wait()
    passed(logit.at[pl.ds(0, NZ * NX - 1)], gr)
    table = logit[...].reshape(NZ * NX, 128)
    col_top = jnp.max(table, axis=0, keepdims=True)
    col_lse = jnp.log(jnp.sum(jnp.exp(table - col_top), axis=0, keepdims=True)) + col_top
    picked = jnp.where(lane == dp, 0.5 * col_lse - row, 0.0)
    value = 0.5 * row_lse + jnp.sum(picked, axis=1, keepdims=True)
    loss[...] = jnp.broadcast_to(value, (1, 128))
    pltpu.make_async_copy(loss, loss_out, lsem.at[7]).start()
    passed(logit.at[pl.ds(0, NZ * NX - 1)], gs)
    pltpu.make_async_copy(loss, loss_out, lsem.at[7]).wait()


def local(
    queries, keys, values, tokens_in, out_weight, pool_keys, proj_weight, captions, valid_frames
):
    any_ = pl.BlockSpec(memory_space=pl.ANY)
    dma = pltpu.SemaphoreType.DMA
    block_out, loss = pl.pallas_call(
        body,
        out_shape=(
            pltpu.VMEM((TOK, D), BF16),
            pltpu.VMEM((1, 128), F32),
        ),
        in_specs=[any_, any_, any_, any_, any_, any_, any_, any_, any_],
        out_specs=(any_, any_),
        scratch_shapes=[
            pltpu.VMEM((TOK, D), BF16),
            pltpu.VMEM((PIECE, HEADS * HD), BF16),
            pltpu.VMEM((400, 1024), F32),
            pltpu.VMEM((G, D), BF16),
            pltpu.VMEM((1, 1024), F32),
            pltpu.VMEM((1, 1), jnp.int32),
            pltpu.VMEM((TOK, D), BF16),
            pltpu.VMEM((1, 128), F32),
            pltpu.VMEM((NX, 112, 256), BF16),
            pltpu.VMEM((112, 512), BF16),
            pltpu.VMEM((NX, 112, 256), BF16),
            pltpu.VMEM((NX, 112, 512), BF16),
            pltpu.VMEM((416, 512), F32),
            pltpu.VMEM((D, HEADS * HD), BF16),
            pltpu.VMEM((ROUNDS, 3, SEQ, HD), BF16),
            pltpu.VMEM((SEQ, 2 * HD), BF16),
            pltpu.VMEM((SEQ, 2 * HD), BF16),
            pltpu.VMEM((ROUNDS, NF, TOK, HD), BF16),
            pltpu.VMEM((TOK, HEADS * HD), BF16),
            pltpu.VMEM((TOK, D), F32),
            pltpu.VMEM((1, D), F32),
            pltpu.VMEM((NF, 1, 512), F32),
            pltpu.VMEM((NF, 1, 512), F32),
            pltpu.VMEM((1, 8, 128), F32),
            pltpu.VMEM((NF, 8, 128), F32),
            pltpu.VMEM((NZ, NX, 8, 128), F32),
            pltpu.VMEM((NZ * NX, 1, 128), F32),
            dma((8,)),
            dma((ROUNDS,)), dma((ROUNDS,)),
            dma((ROUNDS,)), dma((ROUNDS + 1,)),
            dma, dma((3,)),
            dma, dma((3,)),
            dma, dma((2, 2, 4)),
            dma, dma((2, 2, 4)),
            dma, dma((2, 2, NZ)), dma((2, NZ)),
            dma, dma((9,)),
            dma((2,)), dma((10,)),
            dma, dma,
            dma, dma,
            dma, dma,
        ],
        compiler_params=pltpu.CompilerParams(
            collective_id=0, has_side_effects=True, vmem_limit_bytes=60 * 2**20
        ),
    )(
        queries[0], keys[0], values[0], tokens_in[0], out_weight.T, pool_keys.T, proj_weight, captions,
        valid_frames.reshape(1, 1),
    )
    return block_out[None], loss[0, 0:1]


def solution(mesh):
    placed = (
        P("dp", "frame", None),
        P("dp", "frame", None),
        P("dp", "frame", None),
        P("dp", "frame", None),
        P(None, "dp"),
        P(),
        P("frame", None),
        P("dp", None),
        P("dp"),
    )
    return jax.shard_map(
        local,
        mesh=mesh,
        in_specs=placed,
        out_specs=(P("dp", "frame", None), P("dp")),
        check_vma=False,
    )
```

```python
import functools

import jax
import jax.numpy as jnp
from jax import lax
from jax.experimental import pallas as pl
from jax.experimental.pallas import tpu as pltpu
from jax.sharding import PartitionSpec as P

D = 3200
HEADS = 24
HD = 128
G = 16
TPF = 128
SEQ = 2048
TOK = 256
ROUNDS = 3
NF = 8
NZ = 8
NX = 4
KR = NF * HD
TILE_AT = (0, 2 * KR)
HALF_AT = KR
PIECE = 100
SCALE = 1.4426950408889634 / (128.0**0.5)
SHARP = 1.0 / 0.07
FAR_FIRST = (4, 3, 5, 2, 6, 1, 7)

MESH = pl.DeviceIdType.MESH
F32 = jnp.float32
BF16 = jnp.bfloat16


def nt_dot(a, b):
    return lax.dot_general(a, b, (((1,), (1,)), ((), ())), preferred_element_type=F32)


def body(
    q_hbm, k_hbm, v_hbm, tok_hbm, w_hbm, pk_hbm, proj_hbm, cap_hbm, valid_hbm,
    out_ref, loss_out,
    tok, wown, proj, pool, cap, count, blk, loss, own_a, own_x, stage_a, stage_x, m32, wt, qkv, k2, vlive, osend, orecv, acc,
    msg, pout, parts, emb, embs, caps, logit,
    lsem, qs, qr, os_, or_, as_, ar, x1s, x1r, z1s, z1r, z2s, z2r, x2s, x2r, x2f, sbs, sbr,
    cs, cr, ms, mr, es, er, gs, gr,
):
    dp = lax.axis_index("dp")
    f = lax.axis_index("frame")
    z = dp // NX
    x = lax.rem(dp, NX)
    c = lax.rem(f, 2)
    sib = f + 1 - 2 * c
    sign = 1 - 2 * c
    right = lax.rem(x + 1, NX)
    left = lax.rem(x + NX - 1, NX)
    across = lax.rem(x + 2, NX)

    def at_z(zz):
        return {"dp": zz * NX + x}

    def at_x(xx):
        return {"dp": z * NX + xx}

    def remote(src, dst, ssem, rsem, where):
        return pltpu.make_async_remote_copy(
            src_ref=src, dst_ref=dst, send_sem=ssem, recv_sem=rsem, device_id=where, device_id_type=MESH
        )

    def passed(ref, sem):
        pltpu.make_async_copy(ref, ref, sem).wait()

    loads = [
        pltpu.make_async_copy(w_hbm, wown, lsem.at[0]),
        pltpu.make_async_copy(tok_hbm, tok, lsem.at[1]),
        pltpu.make_async_copy(cap_hbm, cap, lsem.at[2]),
        pltpu.make_async_copy(proj_hbm, proj, lsem.at[3]),
        pltpu.make_async_copy(pk_hbm, pool, lsem.at[4]),
        pltpu.make_async_copy(valid_hbm, count, lsem.at[5]),
    ]
    for load in loads:
        load.start()

    barrier = pltpu.get_barrier_semaphore()
    for i in range(1, NF):
        pl.semaphore_signal(barrier, inc=1, device_id={"frame": lax.rem(f + i, NF)}, device_id_type=MESH)
    for i in range(1, NX):
        pl.semaphore_signal(barrier, inc=1, device_id=at_x(lax.rem(x + i, NX)), device_id_type=MESH)
    for i in range(1, NZ):
        pl.semaphore_signal(barrier, inc=1, device_id=at_z(lax.rem(z + i, NZ)), device_id_type=MESH)

    half = pl.multiple_of(c * 512, 512)
    pl.semaphore_wait(barrier, NF - 1 + NX - 1 + NZ - 1)

    def a_copy(i, src):
        to = lax.rem(x + i, NX)
        return remote(own_a.at[to], stage_a.at[src], as_, ar.at[i - 1], at_x(to))

    def x1_copy(i, src):
        return remote(own_x, stage_x.at[src], x1s, x1r.at[i - 1], at_x(lax.rem(x + i, NX)))

    def owner_lanes(tile, xx):
        return pl.ds(pl.multiple_of(TILE_AT[tile] + half + xx * 128, 128), 128)

    def half_lanes(h):
        return pl.ds(pl.multiple_of(HALF_AT + half + 256 * h, 256), 256)

    def block_rows(zb):
        return pl.ds(pl.multiple_of(400 * zb, 16), 400)

    def zmove(part, way, step):
        s = sign if way == part else -sign
        return lax.rem(z - s * step + NZ, NZ)

    def znext(part, way):
        s = sign if way == part else -sign
        return lax.rem(z + s + NZ, NZ)

    LAST = (4, 3)

    def z2_copy(tile, way, step, sem_step):
        ref = wt.at[block_rows(zmove(tile, way, step)), owner_lanes(tile, x)]
        return remote(ref, ref, z2s, z2r.at[tile, way, sem_step], at_z(znext(tile, way)))

    def z1_copy(h, way, step, sem_step):
        ref = wt.at[block_rows(zmove(h, way, step)), half_lanes(h)]
        return remote(ref, ref, z1s, z1r.at[h, way, sem_step], at_z(znext(h, way)))

    def place(tile, o):
        return zmove(tile, 0, (o + 1) // 2) if o % 2 else zmove(tile, 1, o // 2)

    def x2_copy(tile, way, o, xx):
        ref = wt.at[block_rows(place(tile, o)), owner_lanes(tile, xx)]
        return remote(ref, ref, x2s, x2r.at[tile, way, o], at_x(right if way == 0 else left))

    def x2_forward_copy(tile, way, o, xx):
        ref = wt.at[block_rows(place(tile, o)), owner_lanes(tile, xx)]
        return remote(ref, ref, x2s, x2f.at[tile, o], at_x(right if way == 0 else left))

    def x2_own(tile, o):
        x2_copy(tile, 0, o, x).start()
        x2_copy(tile, 1, o, x).start()

    def x2_forward(tile, o):
        way, xx = ((0, left), (1, right))[o % 2]
        x2_copy(tile, way, o, xx).wait_recv()
        x2_forward_copy(tile, way, o, xx).start()

    def x2_near(tile):
        for o in range(NZ):
            way, xx = ((1, right), (0, left))[o % 2]
            x2_copy(tile, way, o, xx).wait_recv()

    def x2_far(tile):
        for o in range(NZ):
            x2_forward_copy(tile, o % 2, o, across).wait_recv()

    def z2_start(tile):
        for way in range(2):
            z2_copy(tile, way, 0, 0).start()

    def z2_step(tile, step):
        for way in range(2):
            if step <= LAST[way]:
                z2_copy(tile, way, step, step - 1).wait_recv()
                if step < LAST[way]:
                    z2_copy(tile, way, step, step).start()
                x2_own(tile, 2 * step - 1 if way == 0 else 2 * step)

    def z1_start(h):
        for way in range(2):
            z1_copy(h, way, 0, 0).start()

    def z1_step(h, step):
        for way in range(2):
            if step <= LAST[way]:
                z1_copy(h, way, step, step - 1).wait_recv()
                if step < LAST[way]:
                    z1_copy(h, way, step, step).start()

    def sib_copy(which, core):
        base = core * 512
        if which == 0:
            lanes = pl.ds(pl.multiple_of(HALF_AT + base, 512), 512)
        else:
            tile, nth = divmod(which - 1, 4)
            xx = (x, left, right, across)[nth]
            lanes = pl.ds(pl.multiple_of(TILE_AT[tile] + base + xx * 128, 128), 128)
        ref = wt.at[:, lanes]
        return remote(ref, ref, sbs, sbr.at[which], {"frame": sib})

    def sib_start(which):
        sib_copy(which, c).start()

    def sib_wait(which):
        sib_copy(which, 1 - c).wait_recv()

    def merge_a():
        stage_a[x] = own_a[x]
        for i in range(1, NX):
            a_copy(i, lax.rem(x - i + NX, NX)).wait_recv()
        for i in range(NX):
            m32[PIECE * i : PIECE * i + 112, 0:256] = stage_a[i].astype(F32)
        for tile in range(2):
            wt[block_rows(z), owner_lanes(tile, x)] = m32[0:400, 128 * tile : 128 * (tile + 1)].astype(BF16)

    def merge_x():
        stage_x[x] = own_x[...]
        for i in range(1, NX):
            x1_copy(i, lax.rem(x - i + NX, NX)).wait_recv()
        for i in range(NX):
            m32[PIECE * i : PIECE * i + 112, :] = stage_x[i].astype(F32)
        wt[block_rows(z), pl.ds(pl.multiple_of(HALF_AT + half, 512), 512)] = m32[0:400, :].astype(BF16)

    def qkv_start(r):
        for i in range(1, NF):
            t = lax.rem(f + i, NF)
            cols = pl.ds(pl.multiple_of((r * NF + t) * HD, HD), HD)
            for a, ref in enumerate((k_hbm, v_hbm, q_hbm)):
                remote(
                    ref.at[:, cols],
                    qkv.at[r, a, pl.ds(pl.multiple_of(f * TOK, TOK), TOK), :],
                    qs.at[r], qr.at[r], {"frame": t},
                ).start()
        cols = pl.ds(pl.multiple_of((r * NF + f) * HD, HD), HD)
        for a, ref in enumerate((k_hbm, v_hbm, q_hbm)):
            pltpu.make_async_copy(
                ref.at[:, cols], qkv.at[r, a, pl.ds(pl.multiple_of(f * TOK, TOK), TOK), :], qr.at[r]
            ).start()

    def qkv_wait(r):
        pltpu.make_async_copy(qkv.at[r], qkv.at[r], qr.at[r]).wait()

    def prepare(r, valid):
        for i in range(8):
            rows = slice(256 * i, 256 * (i + 1))
            live = (lax.broadcasted_iota(jnp.int32, (256, HD), 0) + 256 * i) // TPF < valid
            kk = qkv[r, 0, rows, :].astype(F32)
            first = qkv[r, 0, 0:16, :].astype(F32)[0:1, :]
            kk = jnp.where(live, kk, jnp.broadcast_to(first, (256, HD))) * SCALE
            hi = kk.astype(BF16)
            k2[rows, 0:HD] = hi
            k2[rows, HD : 2 * HD] = (kk - hi.astype(F32)).astype(BF16)
            vlive[rows, :] = jnp.where(live, qkv[r, 1, rows, :].astype(F32), 0.0).astype(BF16)

    def attend(r, start, stop, dead):
        for i in range(start, stop):
            b = lax.rem(f + 1 + i, NF)
            qq = qkv[r, 2, pl.ds(pl.multiple_of(b * TOK, TOK), TOK), :]
            scores = nt_dot(jnp.concatenate([qq, qq], axis=1), k2[...])
            peak = jnp.max(scores, axis=1, keepdims=True)
            expo = jnp.exp2(scores - peak)
            total = jnp.sum(expo, axis=1, keepdims=True) - dead * expo[:, 0:1]
            weights = (expo * (1.0 / total)).astype(BF16)
            osend[r, b] = jnp.dot(weights, vlive[...], preferred_element_type=F32).astype(BF16)

    def give_back(r, start, stop):
        group = r + start // 4
        heads = pl.ds(pl.multiple_of(r * KR + f * HD, HD), HD)
        for i in range(start, stop):
            b = lax.rem(f + 1 + i, NF)
            if i < NF - 1:
                remote(osend.at[r, b], orecv.at[:, heads], os_.at[r], or_.at[group], {"frame": b}).start()
            else:
                pltpu.make_async_copy(osend.at[r, b], orecv.at[:, heads], or_.at[group]).start()

    def attended_wait(r):
        cols = orecv.at[:, pl.ds(r * KR, KR)]
        pltpu.make_async_copy(cols, cols, or_.at[r]).wait()

    def blocks_of_columns(step, unroll):
        def one(n, carry):
            return step(pl.ds(pl.multiple_of(n * 1024, 128), 1024), carry)

        return step(pl.ds(3072, 128), lax.fori_loop(0, 3, one, jnp.zeros((G, TOK), F32), unroll=unroll))

    def project(r):
        def step(cols, carry):
            part = nt_dot(orecv[:, r * KR : (r + 1) * KR], wt[cols, r * KR : (r + 1) * KR])
            if r == 0:
                acc[:, cols] = tok[:, cols].astype(F32) + part
            else:
                acc[:, cols] += part
            return carry

        blocks_of_columns(step, False)

    def project_last(group):
        cols = orecv.at[:, pl.ds(0, 4 * HD)]
        pltpu.make_async_copy(cols, cols, or_.at[2 + group]).wait()
        lanes = []
        for i in range(1, 5):
            source = lax.rem(f - i - 4 * group + 2 * NF, NF)
            lanes.append(pl.ds(pl.multiple_of(2 * KR + source * HD, HD), HD))
        rows = jnp.concatenate([orecv[:, ln] for ln in lanes], axis=1)

        def step(cols, carry):
            part = nt_dot(rows, jnp.concatenate([wt[cols, ln] for ln in lanes], axis=1))
            if group == 0:
                acc[:, cols] += part
                return carry
            block = (acc[:, cols] + part).astype(BF16)
            blk[:, cols] = block
            return carry + nt_dot(pool[:, cols], block)

        return blocks_of_columns(step, True)

    qkv_start(0)

    loads[0].wait()
    for to in range(NX):
        for tile in range(2):
            lanes = pl.ds(pl.multiple_of(TILE_AT[tile] + half + to * 128, 128), 128)
            own_a[to, 0:PIECE, 128 * tile : 128 * (tile + 1)] = wown[:, lanes]
    own_x[0:PIECE, :] = wown[:, pl.ds(pl.multiple_of(HALF_AT + half, 512), 512)]
    for to in range(NX):
        own_a[to, 96:112, :] = jnp.concatenate([own_a[to, 96:112, :][0:4], jnp.zeros((12, 256), BF16)], axis=0)
    own_x[96:112, :] = jnp.concatenate([own_x[96:112, :][0:4], jnp.zeros((12, 512), BF16)], axis=0)
    for i in range(1, NX):
        a_copy(i, x).start()
    merge_a()
    z2_start(0)
    z2_start(1)
    for i in range(1, NX):
        x1_copy(i, x).start()
    x2_own(0, 0)
    x2_own(1, 0)
    qkv_start(1)
    qkv_start(2)

    loads[2].wait()
    loads[5].wait()
    valid = count[...]
    dead = (SEQ - TPF * valid).astype(F32)
    for n in range(8):
        emb[0, n : n + 1, :] = cap[0:1, 128 * n : 128 * (n + 1)]
    own_cap = emb[0]
    norm = jnp.sqrt(jnp.sum(own_cap * own_cap, keepdims=True) + 1e-06)
    caps[z, x] = own_cap / norm

    def cap_x(i, xx):
        ref = caps.at[z, xx]
        return remote(ref, ref, cs.at[0], cr.at[i - 1], at_x(lax.rem(x + i, NX)))

    def cap_z(i, zz):
        ref = caps.at[zz]
        return remote(ref, ref, cs.at[1], cr.at[NX - 2 + i], at_z(lax.rem(z + i, NZ)))

    for i in range(1, NX):
        cap_x(i, x).start()

    z2_step(0, 1)
    z2_step(1, 1)
    z2_step(0, 2)
    z2_step(1, 2)
    merge_x()
    z1_start(0)
    z2_step(0, 3)
    z2_step(1, 3)
    z1_start(1)
    for i in range(1, NX):
        cap_x(i, lax.rem(x - i + NX, NX)).wait_recv()
    for i in range(1, NZ):
        cap_z(i, z).start()

    qkv_wait(0)
    prepare(0, valid)
    attend(0, 0, 2, dead)
    z2_step(0, 4)
    z2_step(1, 4)
    z1_step(0, 1)
    attend(0, 2, 6, dead)
    z1_step(1, 1)
    attend(0, 6, 8, dead)
    for o in range(0, 3):
        x2_forward(0, o)
    z1_step(0, 2)
    for o in range(3, 6):
        x2_forward(0, o)

    qkv_wait(1)
    prepare(1, valid)
    attend(1, 0, 2, dead)
    z1_step(1, 2)
    sib_start(1)
    sib_start(5)
    attend(1, 2, 5, dead)
    z1_step(0, 3)
    x2_forward(0, 6)
    x2_forward(0, 7)
    x2_near(0)
    sib_start(2)
    sib_start(3)
    for o in range(0, 4):
        x2_forward(1, o)
    give_back(0, 0, 8)
    attend(1, 5, 8, dead)
    give_back(1, 0, 8)
    z1_step(1, 3)
    for o in range(4, 8):
        x2_forward(1, o)
    x2_near(1)
    sib_start(6)
    sib_start(7)

    qkv_wait(2)
    prepare(2, valid)
    attend(2, 0, 4, dead)
    give_back(2, 0, 4)
    x2_far(0)
    sib_start(4)
    z1_step(0, 4)
    z1_step(1, 4)
    sib_start(0)
    attend(2, 4, 8, dead)
    give_back(2, 4, 8)

    loads[1].wait()
    loads[3].wait()
    loads[4].wait()
    for which in range(1, 5):
        sib_wait(which)
    attended_wait(0)
    project(0)
    x2_far(1)
    sib_start(8)
    sib_wait(0)
    attended_wait(1)
    project(1)
    for i in range(1, NZ):
        cap_z(i, lax.rem(z - i + NZ, NZ)).wait_recv()
    for which in range(5, 9):
        sib_wait(which)
    project_last(0)
    scores = project_last(1)

    token = lax.broadcasted_iota(jnp.int32, (G, TOK), 1) + f * TOK
    live = token // TPF < valid
    masked = jnp.where(live, scores, -1e30)
    peak = jnp.max(masked, axis=1, keepdims=True)
    expo = jnp.where(live, jnp.exp(masked - peak), 0.0)
    total = jnp.sum(expo, axis=1, keepdims=True)
    e0 = expo.astype(BF16)
    rest = expo - e0.astype(F32)
    e1 = rest.astype(BF16)
    e2 = (rest - e1.astype(F32)).astype(BF16)
    w48 = jnp.dot(jnp.concatenate([e0, e1, e2], axis=0), blk[...], preferred_element_type=F32)
    w16 = w48[0:G] + w48[G : 2 * G] + w48[2 * G : 3 * G]
    mine = lax.broadcasted_iota(jnp.int32, (G, D), 1) // (D // G) == lax.broadcasted_iota(jnp.int32, (G, D), 0)

    msg[...] = jnp.sum(jnp.where(mine, w16, 0.0), axis=0, keepdims=True)
    stats = jnp.concatenate([peak, total], axis=1)
    for t in range(NF):
        pout[t, :, 0:400] = msg[:, 400 * t : 400 * (t + 1)]
        pout[t, :, 400:402] = stats[2 * t : 2 * t + 1, :]
        pout[t, :, 402:404] = stats[2 * t + 1 : 2 * t + 2, :]

    def part_copy(i, src):
        t = lax.rem(f + i, NF)
        return remote(pout.at[t], parts.at[src], ms, mr, {"frame": t})

    for i in FAR_FIRST:
        part_copy(i, f).start()
    store = pltpu.make_async_copy(blk, out_ref, lsem.at[6])
    store.start()
    parts[f] = pout[f]

    passed(stage_a.at[pl.ds(0, 3)], as_)
    passed(stage_x.at[pl.ds(0, 3)], x1s)
    passed(wt.at[pl.ds(0, 2800), pl.ds(0, 256)], z2s)
    passed(wt.at[pl.ds(0, 2800), pl.ds(0, 512)], z1s)
    passed(wt.at[:, pl.ds(0, 768)], x2s)
    passed(wt.at[:, pl.ds(0, 1536)], sbs)
    for r in range(ROUNDS):
        passed(qkv.at[r, :, pl.ds(0, SEQ - TOK), :], qs.at[r])
        passed(orecv.at[:, pl.ds(0, KR - HD)], os_.at[r])
    passed(caps.at[0, pl.ds(0, 3)], cs.at[0])
    passed(caps.at[pl.ds(0, 7)], cs.at[1])

    passed(parts.at[pl.ds(0, NF - 1)], mr)
    gathered = parts[...].reshape(NF, 512)
    first = lax.broadcasted_iota(jnp.int32, (NF, 512), 1) < D // G
    peaks = jnp.where(first, gathered[:, 400:401], gathered[:, 402:403])
    totals = jnp.where(first, gathered[:, 401:402], gathered[:, 403:404])
    top = jnp.max(peaks, axis=0, keepdims=True)
    scale = jnp.exp(peaks - top)
    denominator = jnp.sum(totals * scale, axis=0, keepdims=True)
    pooled = jnp.sum(gathered * scale, axis=0, keepdims=True) / denominator
    column = jnp.transpose(jnp.broadcast_to(pooled, (128, 512)))[0:400]
    for n in range(8):
        emb[0, n : n + 1, :] = jnp.sum(column * proj[:, 128 * n : 128 * (n + 1)], axis=0, keepdims=True)

    def emb_copy(i, src):
        return remote(emb.at[0], embs.at[src], es, er, {"frame": lax.rem(f + i, NF)})

    for i in FAR_FIRST:
        emb_copy(i, f).start()
    embs[f] = emb[0]
    passed(embs.at[pl.ds(0, NF - 1)], er)
    raw = jnp.sum(embs[...], axis=0)
    clip = raw / jnp.sqrt(jnp.sum(raw * raw, keepdims=True) + 1e-06)

    products = jnp.sum(caps[...].reshape(NZ * NX, 8, 128) * clip[None], axis=1)
    square = jnp.concatenate([products, jnp.zeros((96, 128), F32)], axis=0)
    row = SHARP * jnp.sum(jnp.transpose(square), axis=0, keepdims=True)
    logit[dp] = row

    def log_copy(i, src):
        ref = logit.at[src]
        to = lax.rem(dp + i, NZ * NX)
        return remote(ref, ref, gs, gr, {"dp": to})

    for i in range(NZ * NX - 1):
        log_copy(1 + (i + 11) % (NZ * NX - 1), dp).start()
    lane = lax.broadcasted_iota(jnp.int32, (1, 128), 1)
    own = jnp.where(lane < NZ * NX, row, -jnp.inf)
    own_top = jnp.max(own, axis=1, keepdims=True)
    row_lse = jnp.log(jnp.sum(jnp.exp(own - own_top), axis=1, keepdims=True)) + own_top
    passed(pout.at[pl.ds(0, 7)], ms)
    passed(embs.at[pl.ds(0, 7)], es)

    store.wait()
    passed(logit.at[pl.ds(0, NZ * NX - 1)], gr)
    table = logit[...].reshape(NZ * NX, 128)
    col_top = jnp.max(table, axis=0, keepdims=True)
    col_lse = jnp.log(jnp.sum(jnp.exp(table - col_top), axis=0, keepdims=True)) + col_top
    picked = jnp.where(lane == dp, 0.5 * col_lse - row, 0.0)
    value = 0.5 * row_lse + jnp.sum(picked, axis=1, keepdims=True)
    loss[...] = jnp.broadcast_to(value, (1, 128))
    pltpu.make_async_copy(loss, loss_out, lsem.at[7]).start()
    passed(logit.at[pl.ds(0, NZ * NX - 1)], gs)
    pltpu.make_async_copy(loss, loss_out, lsem.at[7]).wait()


def local(
    queries, keys, values, tokens_in, out_weight, pool_keys, proj_weight, captions, valid_frames
):
    any_ = pl.BlockSpec(memory_space=pl.ANY)
    dma = pltpu.SemaphoreType.DMA
    block_out, loss = pl.pallas_call(
        body,
        out_shape=(
            pltpu.VMEM((TOK, D), BF16),
            pltpu.VMEM((1, 128), F32),
        ),
        in_specs=[any_, any_, any_, any_, any_, any_, any_, any_, any_],
        out_specs=(any_, any_),
        scratch_shapes=[
            pltpu.VMEM((TOK, D), BF16),
            pltpu.VMEM((PIECE, HEADS * HD), BF16),
            pltpu.VMEM((400, 1024), F32),
            pltpu.VMEM((G, D), BF16),
            pltpu.VMEM((1, 1024), F32),
            pltpu.VMEM((1, 1), jnp.int32),
            pltpu.VMEM((TOK, D), BF16),
            pltpu.VMEM((1, 128), F32),
            pltpu.VMEM((NX, 112, 256), BF16),
            pltpu.VMEM((112, 512), BF16),
            pltpu.VMEM((NX, 112, 256), BF16),
            pltpu.VMEM((NX, 112, 512), BF16),
            pltpu.VMEM((416, 512), F32),
            pltpu.VMEM((D, HEADS * HD), BF16),
            pltpu.VMEM((ROUNDS, 3, SEQ, HD), BF16),
            pltpu.VMEM((SEQ, 2 * HD), BF16),
            pltpu.VMEM((SEQ, HD), BF16),
            pltpu.VMEM((ROUNDS, NF, TOK, HD), BF16),
            pltpu.VMEM((TOK, HEADS * HD), BF16),
            pltpu.VMEM((TOK, D), F32),
            pltpu.VMEM((1, D), F32),
            pltpu.VMEM((NF, 1, 512), F32),
            pltpu.VMEM((NF, 1, 512), F32),
            pltpu.VMEM((1, 8, 128), F32),
            pltpu.VMEM((NF, 8, 128), F32),
            pltpu.VMEM((NZ, NX, 8, 128), F32),
            pltpu.VMEM((NZ * NX, 1, 128), F32),
            dma((8,)),
            dma((ROUNDS,)), dma((ROUNDS,)),
            dma((ROUNDS,)), dma((ROUNDS + 1,)),
            dma, dma((3,)),
            dma, dma((3,)),
            dma, dma((2, 2, 4)),
            dma, dma((2, 2, 4)),
            dma, dma((2, 2, NZ)), dma((2, NZ)),
            dma, dma((9,)),
            dma((2,)), dma((10,)),
            dma, dma,
            dma, dma,
            dma, dma,
        ],
        compiler_params=pltpu.CompilerParams(
            collective_id=0, has_side_effects=True, vmem_limit_bytes=60 * 2**20
        ),
    )(
        queries[0], keys[0], values[0], tokens_in[0], out_weight.T, pool_keys.T, proj_weight, captions,
        valid_frames.reshape(1, 1),
    )
    return block_out[None], loss[0, 0:1]


def solution(mesh):
    placed = (
        P("dp", "frame", None),
        P("dp", "frame", None),
        P("dp", "frame", None),
        P("dp", "frame", None),
        P(None, "dp"),
        P(),
        P("frame", None),
        P("dp", None),
        P("dp"),
    )
    return jax.shard_map(
        local,
        mesh=mesh,
        in_specs=placed,
        out_specs=(P("dp", "frame", None), P("dp")),
        check_vma=False,
    )
```
